128 devices in a mesh: stream: 32 (over x, y, core), span: 4 (over z).
Axes of the slice: x: 4, y: 4, z: 4, core: 2. Of those that a mesh axis runs over, the one named last changes fastest.
Arguments:
- rhs: float32 [512, 32, 5, 128], P('stream', 'span'), may hold values from -0.8 to 0.8
- adjoint: float32 [512, 32, 5, 128], P('stream', 'span'), may hold values from -6 to 6
- diag_x: float32 [512, 32, 5, 5, 128], P('stream', 'span'), may hold values from -0.3 to 0.6
- lower_x: float32 [512, 32, 5, 5, 128], P('stream', 'span'), may hold values from -1 to 1
- upper_x: float32 [512, 32, 5, 5, 128], P('stream', 'span'), may hold values from -1 to 1
- diag_y: float32 [512, 32, 5, 5, 128], P('stream', 'span'), may hold values from -0.3 to 0.6
- lower_y: float32 [512, 32, 5, 5, 128], P('stream', 'span'), may hold values from -1 to 1
- upper_y: float32 [512, 32, 5, 5, 128], P('stream', 'span'), may hold values from -1 to 1
- metric: bfloat16 [512, 32, 3, 5, 128], P('stream', 'span'), may hold values from -0.25 to 0.25
- node_cell: int32 [32, 4, 128], P('stream', 'span'), may hold values from 0 to 127, each once within a row
- node_owner: int32 [32, 4, 128], P('stream', 'span'), may hold values from 0 to 2047
- node_weight: float32 [32, 4, 128], P('stream', 'span'), may hold values from 0.2 to 1
- node_count: int32 [32, 4], P('stream', 'span'), may hold values from 16 to 128, as said below
Outputs:
- adjoint_new: float32 [512, 32, 5, 128], P('stream', 'span')
- control_grad: float32 [3, 2048], P(None, ('stream', 'span'))
The draws below stay inside these ranges and needn't reach their ends.
Inputs may be any that keep to these rules, and one draw needn't show every extreme that they name: `node_cell`: each block's list names every one of its wall cells once. Only the first node_count slots of a block are surface nodes.
All inputs are finite; a program needn't handle non-finite values.
Results may differ from the reference program's by a relative error of at most 0.0003.
Values sent between devices are 32-bit elements; how exact they have to be, the bound alone decides.
No kernel may reach another device: no remote copies, remote signals or barrier semaphores. Data moves between devices by JAX's collectives and lax.ppermute only.
A program may use at most 64 MiB of HBM per device.

```python
import math
import jax
import jax.numpy as jnp
from jax import lax

SX = 16
SY = 8
NN = 128
NX = 512
NY = 32
STREAM_BLOCKS = 32
SPAN_BLOCKS = 4
SLOTS = 128
NCP = 2048


def coupling_draw(key, chain_len, along):
    derived_seed_list = jax.random.split(key, 8)
    device_layout_dims = (NX, NY, NN)
    spread = jax.random.uniform(derived_seed_list[0], device_layout_dims, jnp.float32, 0.5, 1.0)
    relabel = jax.random.permutation(derived_seed_list[1], 5)
    chosen = jax.random.randint(derived_seed_list[2], (), 0, 2).astype(jnp.float32)
    slow_first = chosen
    slow_second = 1.0 - chosen
    slow_rate = math.log(10.0) / (4.0 * chain_len) * spread
    fast_rate = spread / 20.0
    lattice_coordinate = lax.broadcasted_iota(jnp.int32, device_layout_dims, along)
    destination_locations = jax.random.randint(derived_seed_list[3], (3,), 0, chain_len)
    contiguous_count = jnp.any(lattice_coordinate[..., None] == destination_locations, axis=-1)
    magnitude_multiplier = jnp.where(contiguous_count, jax.random.uniform(derived_seed_list[4], device_layout_dims, jnp.float32, 0.5, 0.8), 1.0)
    rate_first = magnitude_multiplier * jnp.exp(-(slow_first * slow_rate + (1.0 - slow_first) * fast_rate))
    rate_second = magnitude_multiplier * jnp.exp(-(slow_second * slow_rate + (1.0 - slow_second) * fast_rate))
    angle_one = jax.random.uniform(derived_seed_list[5], device_layout_dims, jnp.float32, 0.2, 0.6)
    angle_two = jax.random.uniform(derived_seed_list[6], device_layout_dims, jnp.float32, 0.2, 0.6)
    angle_three = jax.random.uniform(derived_seed_list[7], device_layout_dims, jnp.float32, 0.2, 0.6)
    cos_one, sin_one = (jnp.cos(angle_one), jnp.sin(angle_one))
    cos_two, sin_two = (jnp.cos(angle_two), jnp.sin(angle_two))
    cos_three, sin_three = (jnp.cos(angle_three), jnp.sin(angle_three))
    empty = jnp.zeros(device_layout_dims, jnp.float32)
    matrix_rows = [[rate_first * cos_one, -rate_first * sin_one, empty, empty, empty], [rate_first * sin_one, rate_first * cos_one, empty, empty, empty], [empty, empty, rate_second * cos_two, -rate_second * sin_two * cos_three, rate_second * sin_two * sin_three], [empty, empty, rate_second * sin_two, rate_second * cos_two * cos_three, -rate_second * cos_two * sin_three], [empty, empty, empty, rate_second * sin_three, rate_second * cos_three]]
    matrix = jnp.stack([jnp.stack(entries, axis=2) for entries in matrix_rows], axis=2)
    matrix = jnp.take(matrix, relabel, axis=2)
    return jnp.take(matrix, relabel, axis=3)


def diag_block(key):
    derived_seed_list = jax.random.split(key, 2)
    main = jax.random.uniform(derived_seed_list[0], (NX, NY, 5, NN), jnp.float32, 0.2, 0.6)
    off_part = jnp.clip(0.12 * jax.random.normal(derived_seed_list[1], (NX, NY, 5, 5, NN), jnp.float32), -0.3, 0.3)
    unit = jnp.eye(5, dtype=jnp.float32)[:, :, None]
    return off_part * (1.0 - unit) + unit * main[:, :, :, None, :]


def draw_lower_x(key, part):
    key = jax.random.fold_in(key, 1)
    return coupling_draw(key, NX, 0)


def draw_upper_x(key, part):
    key = jax.random.fold_in(key, 2)
    return coupling_draw(key, NX, 0)


def draw_lower_y(key, part):
    key = jax.random.fold_in(key, 3)
    return coupling_draw(key, NY, 1)


def draw_upper_y(key, part):
    key = jax.random.fold_in(key, 4)
    return coupling_draw(key, NY, 1)


def draw_diag_x(key, part):
    key = jax.random.fold_in(key, 5)
    return diag_block(key)


def draw_diag_y(key, part):
    key = jax.random.fold_in(key, 6)
    return diag_block(key)


def draw_node_count(key, part):
    key = jax.random.fold_in(key, 7)
    halvings = jax.random.randint(key, (STREAM_BLOCKS * SPAN_BLOCKS,), 0, 4)
    divisor = jnp.array([1, 2, 4, 8], jnp.int32)[halvings]
    counts = jnp.maximum(SLOTS // divisor, 1)
    counts = counts.at[0].set(SLOTS).at[1].set(max(1, SLOTS // 8))
    return counts.reshape(STREAM_BLOCKS, SPAN_BLOCKS).astype(jnp.int32)


def touch_ends(values, stream_key, smallest, high):
    longest = values.shape.index(max(values.shape))
    spots = []
    for shift in (0, 1):
        where = [jax.random.randint(jax.random.fold_in(stream_key, axis), (), 0, length) for axis, length in enumerate(values.shape)]
        where[longest] = (where[longest] + shift) % values.shape[longest]
        spots.append(tuple(where))
    return values.at[spots[0]].set(smallest).at[spots[1]].set(high)


def shard_levels(stream_key, shape, pieces, smallest, top_value):
    loudness, own = 1.0, jax.random.fold_in(stream_key, 6)
    for axis_at, shards_of in pieces:
        draws = jnp.exp(jax.random.uniform(jax.random.fold_in(own, axis_at), (shards_of,), jnp.float32, smallest / len(pieces), top_value / len(pieces)))
        loudness = loudness * jnp.repeat(draws, shape[axis_at] // shards_of).reshape([-1 if axis == axis_at else 1 for axis in range(len(shape))])
    return loudness


def bell_draw(stream_key, shape, width, limit, shards=(), held_as=jnp.bfloat16):
    values = width * jax.random.normal(stream_key, shape, jnp.float32)
    if shards:
        values = values * shard_levels(stream_key, shape, shards, -0.22, 0.18)
    return jnp.clip(values, -limit, limit).astype(held_as)


def setup_inputs(seed: int = 0) -> dict:
    splits = jax.random.split(jax.random.key(seed), 14)
    rhs = bell_draw(splits[0], (NX, NY, 5, NN), 0.1, 0.8, ((0, 32), (1, 4)), jnp.float32)
    adjoint = bell_draw(splits[1], (NX, NY, 5, NN), 1.0, 6.0, ((0, 32), (1, 4)), jnp.float32)
    diag_x = draw_diag_x(jax.random.fold_in(splits[13], 71), 0)
    lower_x = draw_lower_x(jax.random.fold_in(splits[13], 71), 0)
    upper_x = draw_upper_x(jax.random.fold_in(splits[13], 71), 0)
    diag_y = draw_diag_y(jax.random.fold_in(splits[13], 71), 0)
    lower_y = draw_lower_y(jax.random.fold_in(splits[13], 71), 0)
    upper_y = draw_upper_y(jax.random.fold_in(splits[13], 71), 0)
    metric = bell_draw(splits[8], (NX, NY, 3, 5, NN), (5 * NN) ** -0.5, 0.25, ((0, 32), (1, 4)))
    node_cell = jax.vmap(lambda own: jax.random.permutation(own, SLOTS))(jax.random.split(splits[9], STREAM_BLOCKS * SPAN_BLOCKS)).reshape((STREAM_BLOCKS, SPAN_BLOCKS, SLOTS)).astype(jnp.int32)
    node_owner = touch_ends(jax.random.randint(splits[10], (STREAM_BLOCKS, SPAN_BLOCKS, SLOTS), 0, NCP), jax.random.fold_in(splits[10], 1), 0, NCP - 1).astype(jnp.int32)
    node_weight = jnp.clip(0.2 + 0.8 * jax.random.uniform(splits[11], (STREAM_BLOCKS, SPAN_BLOCKS, SLOTS), jnp.float32) ** shard_levels(splits[11], (STREAM_BLOCKS, SPAN_BLOCKS, SLOTS), ((0, 32), (1, 4)), -0.2, 0.2), 0.2, 1.0)
    node_count = draw_node_count(jax.random.fold_in(splits[13], 71), 0)
    return {"rhs": rhs, "adjoint": adjoint, "diag_x": diag_x, "lower_x": lower_x, "upper_x": upper_x, "diag_y": diag_y, "lower_y": lower_y, "upper_y": upper_y, "metric": metric, "node_cell": node_cell, "node_owner": node_owner, "node_weight": node_weight, "node_count": node_count}


def act_on(matrix, vector):
    return jnp.sum(matrix * vector[..., None, :, :], axis=-2)


def sweep(driving, coupling, reverse):
    def advance(previous, inputs):
        fresh = inputs[0] - act_on(inputs[1], previous)
        return fresh, fresh

    _, states = lax.scan(advance, jnp.zeros(driving.shape[1:], jnp.float32), (driving, coupling), reverse=reverse)
    return states


def reference(rhs, adjoint, diag_x, lower_x, upper_x, diag_y, lower_y, upper_y, metric, node_cell, node_owner, node_weight, node_count):
    forward = sweep(act_on(diag_x, rhs), lower_x, False)
    stream_done = sweep(forward, upper_x, True)
    turned = jnp.swapaxes(stream_done, 0, 1)
    span_forward = sweep(act_on(jnp.swapaxes(diag_y, 0, 1), turned), jnp.swapaxes(lower_y, 0, 1), False)
    update = jnp.swapaxes(sweep(span_forward, jnp.swapaxes(upper_y, 0, 1), True), 0, 1)
    adjoint_new = adjoint + update
    surface = jnp.sum(metric.astype(jnp.float32) * adjoint_new[:, :, None], axis=(3, 4))
    blocked = surface.reshape(STREAM_BLOCKS, SX, SPAN_BLOCKS, SY, 3).transpose(0, 2, 4, 1, 3)
    blocked = blocked.reshape(STREAM_BLOCKS, SPAN_BLOCKS, 3, SLOTS)
    picked = jnp.take_along_axis(blocked, node_cell[:, :, None, :], axis=3)
    in_use = (jnp.arange(SLOTS, dtype=jnp.int32)[None, None, :] < node_count[:, :, None]).astype(jnp.float32)
    node_terms = picked * (node_weight * in_use)[:, :, None, :]
    unrolled_summands = node_terms.transpose(0, 1, 3, 2).reshape(-1, 3)
    control = jax.ops.segment_sum(unrolled_summands, node_owner.reshape(-1), num_segments=NCP)
    return adjoint_new, control.T
```

```python
import jax
import jax.numpy as jnp
from jax import lax
from jax.experimental import pallas as pl
from jax.experimental.pallas import tpu as pltpu
from jax.sharding import PartitionSpec as P

SX, SY, NN = 16, 8, 128
XS = 32
ROWS = 24
VMEM = 56 * 1024 * 1024


def act(m, v):
    out = []
    for a in range(5):
        t = m[5 * a] * v[0]
        for b in range(1, 5):
            t = t + m[5 * a + b] * v[b]
        out.append(t)
    return out


def act_cols(m, f):
    cols = [act(m, [f[5 * b + c] for b in range(5)]) for c in range(5)]
    return [cols[c][a] for a in range(5) for c in range(5)]


def add(p, q):
    return [x + y for x, y in zip(p, q)]


def sub(p, q):
    return [x - y for x, y in zip(p, q)]


def lanes_quarter(shape):
    return lax.shift_right_logical(lax.broadcasted_iota(jnp.int32, shape, 1), 5)


def maps_kernel(z_ref, rhs, dx, lx, ux, ly, uy, msg, driven, mats, matsel, fs, gs, fy):
    def tiles(ref, i, n=25):
        return [ref[i, k] for k in range(n)]

    def put(ref, i, vals):
        for k, v in enumerate(vals):
            ref[i, k] = v

    d = act(tiles(dx, 0), tiles(rhs, 0, 5))
    put(driven, 0, d)
    put(gs, 0, d)
    f = tiles(lx, 0)
    put(fs, 0, f)

    def fore(i, carry):
        g, f = carry
        l = tiles(lx, i)
        d = act(tiles(dx, i), tiles(rhs, i, 5))
        put(driven, i, d)
        g = sub(d, act(l, g))
        put(gs, i, g)
        f = act_cols(l, f)
        put(fs, i, f)
        return g, f

    g, f = lax.fori_loop(1, SX, fore, (d, f))

    def back(k, carry):
        i = SX - 2 - k
        b, c = carry
        u = tiles(ux, i)
        b = sub(tiles(gs, i, 5), act(u, b))
        c = add(tiles(fs, i), act_cols(u, c))
        return b, c

    b, c = lax.fori_loop(0, SX - 1, back, (g, f))

    def back_map(k, bm):
        return act_cols(tiles(ux, SX - 2 - k), bm)

    bm = lax.fori_loop(0, SX - 1, back_map, tiles(ux, SX - 1))
    zero = jnp.zeros((SY, NN), jnp.float32)
    values = f + g + bm + b + [-x for x in c] + [zero] * 3
    quarter = lanes_quarter((SY, NN))
    for r in range(22):
        four = values[4 * r : 4 * r + 4]
        for nq in range(4):
            out = None
            for kk in range(4):
                shift = (32 * (kk - nq)) % 128
                part = four[kk] if shift == 0 else pltpu.roll(four[kk], shift, 1)
                out = part if out is None else jnp.where(quarter == kk, part, out)
            msg[pl.ds(nq * 8 * ROWS + r, 8, ROWS), :] = out
    for r in range(22, ROWS):
        for nq in range(4):
            msg[pl.ds(nq * 8 * ROWS + r, 8, ROWS), :] = zero

    last = z_ref[0] == 3
    for h in range(2):
        def turned(ref, y):
            return [ref[pl.ds(h * 1600 + k * 8 + y, 8, 200), :] for k in range(25)]

        f = turned(ly, 0)
        put(fy, 0, f)

        def fore_y(y, f):
            f = act_cols(turned(ly, y), f)
            put(fy, y, f)
            return f

        f = lax.fori_loop(1, SY, fore_y, f)
        for k in range(25):
            mats[k, pl.ds(h * 8, 8), :] = f[k]

        def back_y(k, c):
            y = SY - 2 - k
            return add(tiles(fy, y), act_cols(turned(uy, y), c))

        c = lax.fori_loop(0, SY - 1, back_y, f)
        for k in range(25):
            mats[50 + k, pl.ds(h * 8, 8), :] = -c[k]
            matsel[k, pl.ds(h * 8, 8), :] = jnp.where(last, -c[k], mats[k, pl.ds(h * 8, 8), :])

        def back_map_y(k, bm):
            return act_cols(turned(uy, SY - 2 - k), bm)

        bm = lax.fori_loop(0, SY - 1, back_map_y, turned(uy, SY - 1))
        for k in range(25):
            mats[25 + k, pl.ds(h * 8, 8), :] = bm[k]


def solve_kernel(got, out, un, fin, sin):
    un[0] = got[...]
    for q in range(1, 4):
        for p in range(XS):
            un[q, p] = pltpu.roll(got[p], 128 - 32 * q, 1)

    def val(p, k):
        return un[k % 4, p, (k // 4) : (k // 4) + 1, :]

    zero = [jnp.zeros((1, NN), jnp.float32)] * 5

    def fore(p, f):
        for j in range(5):
            fin[p, j : j + 1, :] = f[j]
        return add(act([val(p, k) for k in range(25)], f), [val(p, 25 + j) for j in range(5)])

    lax.fori_loop(0, XS, fore, zero)

    def back(k, s):
        p = XS - 1 - k
        for j in range(5):
            sin[p, j : j + 1, :] = s[j]
        f = [fin[p, j : j + 1, :] for j in range(5)]
        known = add(act([val(p, 60 + k) for k in range(25)], f), [val(p, 55 + j) for j in range(5)])
        return add(known, act([val(p, 30 + k) for k in range(25)], s))

    lax.fori_loop(0, XS, back, zero)
    quarter = lanes_quarter((8, NN))
    for p in range(XS):
        out[p] = jnp.where(quarter == 0, fin[p], pltpu.roll(sin[p], 32, 1))


def replay_kernel(got, driven, lx, ux, dy, ly, uy, dturn, vec, fs, sd, gt):
    quarter = lanes_quarter((SY, NN))

    def entering(j, at):
        out = None
        for nq in range(4):
            part = got[pl.ds(nq * 64 + j, 8, 8), :]
            shift = (32 * nq - 32 * at) % 128
            part = part if shift == 0 else pltpu.roll(part, shift, 1)
            out = part if out is None else jnp.where(quarter == nq, part, out)
        return out

    def tiles(ref, i, n=25):
        return [ref[i, k] for k in range(n)]

    def fore(i, f):
        f = sub(tiles(driven, i, 5), act(tiles(lx, i), f))
        for a in range(5):
            fs[i, a] = f[a]
        return f

    lax.fori_loop(0, SX, fore, [entering(j, 0) for j in range(5)])

    def back(k, s):
        i = SX - 1 - k
        s = sub(tiles(fs, i, 5), act(tiles(ux, i), s))
        d = act(tiles(dy, i), s)
        for a in range(5):
            sd[pl.ds(pl.multiple_of((i * 5 + a) * 8, 8), 8), :] = d[a]
        return s

    lax.fori_loop(0, SX, back, [entering(j, 1) for j in range(5)])

    for h in range(2):
        def turned(ref, y):
            return [ref[pl.ds(h * 1600 + k * 8 + y, 8, 200), :] for k in range(25)]

        g = None
        for y in range(SY):
            d = [sd[pl.ds(h * 320 + a * 8 + y, 8, 40), :] for a in range(5)]
            for a in range(5):
                dturn[y, a, pl.ds(h * 8, 8), :] = d[a]
            g = d if g is None else sub(d, act(turned(ly, y), g))
            for a in range(5):
                gt[y, a] = g[a]
        for a in range(5):
            vec[a, pl.ds(h * 8, 8), :] = g[a]
        b = g
        for y in range(SY - 2, -1, -1):
            b = sub([gt[y, a] for a in range(5)], act(turned(uy, y), b))
        for a in range(5):
            vec[5 + a, pl.ds(h * 8, 8), :] = b[a]


def finish_kernel(z_ref, count, v1, v2, v3, m1, m2, m3, dturn, ly, uy, adjoint, metric, cell, owner,
                  weight, new, part, fin, sin, ft, ut, pk):
    z = z_ref[0]
    halves = [pl.ds(0, 8), pl.ds(8, 8)]
    zero = jnp.zeros((8, NN), jnp.float32)

    def a_of(v, h):
        return [v[j, halves[h], :] for j in range(5)]

    def b_of(v, h):
        return [v[5 + j, halves[h], :] for j in range(5)]

    def mat(m, at, h):
        return [m[25 * at + k, halves[h], :] for k in range(25)]

    def put_in(h, f):
        for j in range(5):
            fin[j, halves[h], :] = f[j]

    for h in range(2):
        @pl.when(z == 0)
        def _():
            put_in(h, [zero] * 5)

        @pl.when(z == 1)
        def _():
            put_in(h, a_of(v3, h))

        @pl.when(z == 2)
        def _():
            put_in(h, add(a_of(v3, h), act(mat(m3, 0, h), a_of(v2, h))))

        @pl.when(z == 3)
        def _():
            f = add(a_of(v2, h), act(mat(m2, 0, h), a_of(v1, h)))
            put_in(h, add(a_of(v3, h), act(mat(m3, 0, h), f)))

    def turned(ref, y, h):
        return [ref[pl.ds(h * 1600 + k * 8 + y, 8, 200), :] for k in range(25)]

    for h in range(2):
        f = [fin[j, halves[h], :] for j in range(5)]
        for y in range(SY):
            f = sub([dturn[y, a, halves[h], :] for a in range(5)], act(turned(ly, y, h), f))
            for a in range(5):
                ft[y, a, halves[h], :] = f[a]

    def put_back(h, s):
        for j in range(5):
            sin[j, halves[h], :] = s[j]

    for h in range(2):
        def own(h=h):
            return [ft[SY - 1, a, halves[h], :] for a in range(5)]

        @pl.when(z == 0)
        def _():
            f1 = own()
            f2 = add(a_of(v1, h), act(mat(m1, 0, h), f1))
            f3 = add(a_of(v2, h), act(mat(m2, 0, h), f2))
            s3 = add(b_of(v3, h), act(mat(m3, 0, h), f3))
            s2 = add(add(b_of(v2, h), act(mat(m2, 2, h), f2)), act(mat(m2, 1, h), s3))
            put_back(h, add(add(b_of(v1, h), act(mat(m1, 2, h), f1)), act(mat(m1, 1, h), s2)))

        @pl.when(z == 1)
        def _():
            f2 = own()
            f3 = add(a_of(v1, h), act(mat(m1, 0, h), f2))
            s3 = add(b_of(v2, h), act(mat(m2, 2, h), f3))
            put_back(h, add(add(b_of(v1, h), act(mat(m1, 2, h), f2)), act(mat(m1, 1, h), s3)))

        @pl.when(z == 2)
        def _():
            put_back(h, add(b_of(v1, h), act(mat(m1, 2, h), own())))

        @pl.when(z == 3)
        def _():
            put_back(h, [zero] * 5)

    for h in range(2):
        s = [sin[j, halves[h], :] for j in range(5)]
        for y in range(SY - 1, -1, -1):
            s = sub([ft[y, a, halves[h], :] for a in range(5)], act(turned(uy, y, h), s))
            for a in range(5):
                ut[pl.ds((y * 5 + a) * 16 + h * 8, 8), :] = s[a]

    for x in range(SX):
        fresh = []
        for a in range(5):
            fresh.append(adjoint[x, a] + ut[pl.ds(a * 16 + x, 8, 80), :])
            new[x, a] = fresh[a]
        for k in range(3):
            t = metric[x, 5 * k].astype(jnp.float32) * fresh[0]
            for a in range(1, 5):
                t = t + metric[x, 5 * k + a].astype(jnp.float32) * fresh[a]
            pk[k, pl.ds(x * 8, 8), :] = t

    row = lax.broadcasted_iota(jnp.int32, (128, 128), 0)
    lane = lax.broadcasted_iota(jnp.int32, (128, 128), 1)
    here = cell[...] == row
    used = jnp.logical_and(here, lane < count[0])
    w = jnp.sum(jnp.where(used, weight[...], 0.0), axis=1, keepdims=True)
    who = jnp.sum(jnp.where(here, owner[...].astype(jnp.float32), 0.0), axis=1, keepdims=True)
    who = who.astype(jnp.int32)
    surface = [jnp.sum(pk[k], axis=1, keepdims=True) * w for k in range(3)]
    which = lax.shift_right_logical(lane, 4)
    picked = jnp.where(which == 0, surface[0], jnp.where(which == 1, surface[1], surface[2]))
    picked = jnp.where(jnp.logical_and(lane < 48, (lane & 15) == (who & 15)), picked, 0.0)
    target = (lax.shift_right_logical(who, 4) == lane).astype(jnp.float32)
    part[...] = lax.dot_general(target, picked, (((0,), (0,)), ((), ())),
                                precision=lax.Precision.HIGHEST, preferred_element_type=jnp.float32)


def call(kernel, outs, scratch, smem=0, n_in=0):
    f32 = jnp.float32
    return pl.pallas_call(
        kernel,
        out_shape=[jax.ShapeDtypeStruct(s, f32) for s in outs],
        in_specs=[pl.BlockSpec(memory_space=pltpu.SMEM)] * smem
        + [pl.BlockSpec(memory_space=pltpu.VMEM)] * (n_in - smem),
        out_specs=[pl.BlockSpec(memory_space=pltpu.VMEM)] * len(outs),
        scratch_shapes=[pltpu.VMEM(s, f32) for s in scratch],
        compiler_params=pltpu.CompilerParams(vmem_limit_bytes=VMEM),
    )


def shards(rhs, adjoint, diag_x, lower_x, upper_x, diag_y, lower_y, upper_y, metric, node_cell,
           node_owner, node_weight, node_count):
    def blocks(m):
        return m.transpose(0, 2, 3, 1, 4).reshape(SX, -1, SY, NN)

    rhs = rhs.transpose(0, 2, 1, 3)
    adjoint = adjoint.transpose(0, 2, 1, 3)
    dx, lx, ux, dy = blocks(diag_x), blocks(lower_x), blocks(upper_x), blocks(diag_y)
    ly = blocks(lower_y).reshape(-1, NN)
    uy = blocks(upper_y).reshape(-1, NN)
    metric = blocks(metric)
    z = lax.axis_index("span").astype(jnp.int32).reshape(1)

    tile = (SX, 25, SY, NN)
    msg, driven, mats, matsel = call(
        maps_kernel,
        [(XS * ROWS, NN), (SX, 5, SY, NN), (75, SX, NN), (25, SX, NN)],
        [tile, (SX, 5, SY, NN), (SY, 25, 8, NN)],
        smem=1, n_in=7,
    )(z, rhs, dx, lx, ux, ly, uy)
    m1 = lax.ppermute(mats, "span", [(1, 0), (2, 1), (3, 2)])
    m2 = lax.ppermute(mats, "span", [(2, 0), (3, 1), (1, 3)])
    m3 = lax.ppermute(matsel, "span", [(3, 0), (1, 2), (2, 3)])
    got = lax.all_to_all(msg.reshape(XS, ROWS, NN), "stream", 0, 0, tiled=True)
    (back,) = call(
        solve_kernel, [(XS, 8, NN)],
        [(4, XS, ROWS, NN), (XS, 8, NN), (XS, 8, NN)], n_in=1,
    )(got)
    back = lax.all_to_all(back, "stream", 0, 0, tiled=True)
    dturn, vec = call(
        replay_kernel,
        [(SY, 5, SX, NN), (10, SX, NN)],
        [(SX, 5, SY, NN), (SX * 5 * SY, NN), (SY, 5, 8, NN)],
        n_in=7,
    )(back.reshape(XS * 8, NN), driven, lx, ux, dy, ly, uy)
    v = [lax.ppermute(vec, "span", [((i + s) % 4, i) for i in range(4)]) for s in (1, 2, 3)]
    new, part = call(
        finish_kernel,
        [(SX, 5, SY, NN), (128, NN)],
        [(5, SX, NN), (5, SX, NN), (SY, 5, SX, NN), (SY * 5 * SX, NN), (3, 128, NN)],
        smem=2, n_in=16,
    )(z, node_count.reshape(1), *v, m1, m2, m3, dturn, ly, uy, adjoint, metric,
      node_cell.reshape(1, -1), node_owner.reshape(1, -1), node_weight.reshape(1, -1))
    parts = lax.all_to_all(part, ("stream", "span"), 0, 0, tiled=True)
    control = jnp.sum(parts, axis=0)[:48].reshape(3, 16)
    return new.transpose(0, 2, 1, 3), control


def solution(mesh):
    cells, mats = P("stream", "span", None, None), P("stream", "span", None, None, None)
    slots = P("stream", "span", None)
    return jax.shard_map(
        shards,
        mesh=mesh,
        in_specs=(cells,) * 2 + (mats,) * 7 + (slots,) * 3 + (P("stream", "span"),),
        out_specs=(cells, P(None, ("stream", "span"))),
        check_vma=False,
    )
```

```python
import jax
import jax.numpy as jnp
from jax import lax
from jax.experimental import pallas as pl
from jax.experimental.pallas import tpu as pltpu
from jax.sharding import PartitionSpec as P

SX, SY, NN = 16, 8, 128
XS = 32
ROWS = 24


def act(m, v):
    out = []
    for a in range(5):
        t = m[5 * a] * v[0]
        for b in range(1, 5):
            t = t + m[5 * a + b] * v[b]
        out.append(t)
    return out


def act_cols(m, f):
    cols = [act(m, [f[5 * b + c] for b in range(5)]) for c in range(5)]
    return [cols[c][a] for a in range(5) for c in range(5)]


def add(p, q):
    return [x + y for x, y in zip(p, q)]


def sub(p, q):
    return [x - y for x, y in zip(p, q)]


def lanes_quarter(shape):
    return lax.shift_right_logical(lax.broadcasted_iota(jnp.int32, shape, 1), 5)


def tiles(ref, i, n=25):
    return [ref[i, k] for k in range(n)]


def put(ref, i, vals):
    for k, v in enumerate(vals):
        ref[i, k] = v


def copies(pairs, sems):
    out = [pltpu.make_async_copy(src, dst, sems.at[k]) for k, (src, dst) in enumerate(pairs)]
    for c in out:
        c.start()
    return out


STEP = 4


def stream_kernel(rhs_h, dx_h, lx_h, ux_h, msg, driven_h, lx, ux, rhs, dx, fs, gs, driven, sems):
    chunks = [pl.ds(k * STEP, STEP) for k in range(SX // STEP)]
    pairs = []
    for c in chunks:
        pairs += [(lx_h.at[c], lx.at[c]), (dx_h.at[c], dx.at[c]), (rhs_h.at[c], rhs.at[c])]
    flight = copies(pairs + [(ux_h, ux)], sems)

    def fore(i, carry):
        g, f = carry
        l = tiles(lx, i)
        d = act(tiles(dx, i), tiles(rhs, i, 5))
        put(driven, i, d)
        g = sub(d, act(l, g))
        put(gs, i, g)
        f = act_cols(l, f)
        put(fs, i, f)
        return g, f

    for k in range(len(chunks)):
        for c in flight[3 * k : 3 * k + 3]:
            c.wait()
        if k == 0:
            g = act(tiles(dx, 0), tiles(rhs, 0, 5))
            put(driven, 0, g)
            put(gs, 0, g)
            f = tiles(lx, 0)
            put(fs, 0, f)
        g, f = lax.fori_loop(max(1, STEP * k), STEP * k + STEP, fore, (g, f))
    kept = pltpu.make_async_copy(driven, driven_h, sems.at[13])
    kept.start()
    flight[-1].wait()

    def back(k, carry):
        i = SX - 2 - k
        b, c = carry
        u = tiles(ux, i)
        b = sub(tiles(gs, i, 5), act(u, b))
        c = add(tiles(fs, i), act_cols(u, c))
        return b, c

    b, c = lax.fori_loop(0, SX - 1, back, (g, f))

    def back_map(k, bm):
        return act_cols(tiles(ux, SX - 2 - k), bm)

    bm = lax.fori_loop(0, SX - 1, back_map, tiles(ux, SX - 1))
    zero = jnp.zeros((SY, NN), jnp.float32)
    values = f + g + bm + b + [-x for x in c] + [zero] * 3
    quarter = lanes_quarter((SY, NN))
    for r in range(22):
        four = values[4 * r : 4 * r + 4]
        for nq in range(4):
            out = None
            for kk in range(4):
                shift = (32 * (kk - nq)) % 128
                part = four[kk] if shift == 0 else pltpu.roll(four[kk], shift, 1)
                out = part if out is None else jnp.where(quarter == kk, part, out)
            msg[pl.ds(nq * 8 * ROWS + r, 8, ROWS), :] = out
    for r in range(22, ROWS):
        for nq in range(4):
            msg[pl.ds(nq * 8 * ROWS + r, 8, ROWS), :] = zero
    kept.wait()


def span_kernel(ly, uy_h, after, mats, fy, uy, sems):
    del after
    (flight,) = copies([(uy_h, uy)], sems)
    def turned(ref, h, y):
        return [ref[pl.ds(h * 1600 + k * 8 + y, 8, 200), :] for k in range(25)]

    for h in range(2):
        f = turned(ly, h, 0)
        put(fy, 8 * h, f)

        def fore_y(y, f):
            f = act_cols(turned(ly, h, y), f)
            put(fy, 8 * h + y, f)
            return f

        f = lax.fori_loop(1, SY, fore_y, f)
        for k in range(25):
            mats[k, pl.ds(h * 8, 8), :] = f[k]
    flight.wait()
    for h in range(2):
        def back_y(k, c):
            y = SY - 2 - k
            return add(tiles(fy, 8 * h + y), act_cols(turned(uy, h, y), c))

        c = lax.fori_loop(0, SY - 1, back_y, tiles(fy, 8 * h + SY - 1))
        for k in range(25):
            mats[50 + k, pl.ds(h * 8, 8), :] = -c[k]

        def back_map_y(k, bm):
            return act_cols(turned(uy, h, SY - 2 - k), bm)

        bm = lax.fori_loop(0, SY - 1, back_map_y, turned(uy, h, SY - 1))
        for k in range(25):
            mats[25 + k, pl.ds(h * 8, 8), :] = bm[k]


def solve_kernel(z_ref, got, mats, out, matsel, un, fin, sin, sems):
    at = jnp.where(z_ref[0] == 3, 50, 0)
    chosen = pltpu.make_async_copy(mats.at[pl.ds(at, 25)], matsel, sems.at[0])
    chosen.start()

    un[0] = got[...]
    for q in range(1, 4):
        for p in range(XS):
            un[q, p] = pltpu.roll(got[p], 128 - 32 * q, 1)

    def val(p, k):
        return un[k % 4, p, (k // 4) : (k // 4) + 1, :]

    zero = [jnp.zeros((1, NN), jnp.float32)] * 5

    def fore(p, f):
        for j in range(5):
            fin[p, j : j + 1, :] = f[j]
        return add(act([val(p, k) for k in range(25)], f), [val(p, 25 + j) for j in range(5)])

    lax.fori_loop(0, XS, fore, zero, unroll=8)

    def back(k, s):
        p = XS - 1 - k
        for j in range(5):
            sin[p, j : j + 1, :] = s[j]
        f = [fin[p, j : j + 1, :] for j in range(5)]
        known = add(act([val(p, 60 + k) for k in range(25)], f), [val(p, 55 + j) for j in range(5)])
        return add(known, act([val(p, 30 + k) for k in range(25)], s))

    lax.fori_loop(0, XS, back, zero, unroll=8)
    quarter = lanes_quarter((8, NN))
    for p in range(XS):
        out[p] = jnp.where(quarter == 0, fin[p], pltpu.roll(sin[p], 32, 1))
    chosen.wait()


def replay_kernel(count, got, cell, owner, weight, ly, driven_h, lx_h, ux_h, dy_h, uy_h, dturn, vec, target,
                  spread, uy, driven, lx, ux, dy, fs, sd, gt, sems):
    chunks = [pl.ds(k * STEP, STEP) for k in range(SX // STEP)]
    pairs = []
    for c in chunks:
        pairs += [(lx_h.at[c], lx.at[c]), (driven_h.at[c], driven.at[c])]
    for c in chunks[::-1]:
        pairs += [(ux_h.at[c], ux.at[c]), (dy_h.at[c], dy.at[c])]
    flight = copies(pairs + [(uy_h, uy)], sems)

    row = lax.broadcasted_iota(jnp.int32, (128, 128), 0)
    lane = lax.broadcasted_iota(jnp.int32, (128, 128), 1)
    here = cell[...] == row
    used = jnp.logical_and(here, lane < count[0])
    w = jnp.sum(jnp.where(used, weight[...], 0.0), axis=1, keepdims=True)
    who = jnp.sum(jnp.where(here, owner[...].astype(jnp.float32), 0.0), axis=1, keepdims=True)
    who = who.astype(jnp.int32)
    target[...] = (lax.shift_right_logical(who, 4) == lane).astype(jnp.float32).T
    mine = jnp.logical_and(lane < 96, (lane & 15) == (who & 15))
    spread[...] = jnp.where(mine, w, 0.0)


    quarter = lanes_quarter((SY, NN))

    def entering(j, at):
        out = None
        for nq in range(4):
            part = got[pl.ds(nq * 64 + j, 8, 8), :]
            shift = (32 * nq - 32 * at) % 128
            part = part if shift == 0 else pltpu.roll(part, shift, 1)
            out = part if out is None else jnp.where(quarter == nq, part, out)
        return out

    def fore(i, f):
        f = sub(tiles(driven, i, 5), act(tiles(lx, i), f))
        for a in range(5):
            fs[i, a] = f[a]
        return f

    f = [entering(j, 0) for j in range(5)]
    for k in range(len(chunks)):
        for c in flight[2 * k : 2 * k + 2]:
            c.wait()
        f = lax.fori_loop(STEP * k, STEP * k + STEP, fore, f)

    def back(k, s):
        i = SX - 1 - k
        s = sub(tiles(fs, i, 5), act(tiles(ux, i), s))
        d = act(tiles(dy, i), s)
        for a in range(5):
            sd[pl.ds(pl.multiple_of((i * 5 + a) * 8, 8), 8), :] = d[a]
        return s

    s = [entering(j, 1) for j in range(5)]
    for k in range(len(chunks)):
        for c in flight[2 * len(chunks) + 2 * k : 2 * len(chunks) + 2 * k + 2]:
            c.wait()
        s = lax.fori_loop(STEP * k, STEP * k + STEP, back, s)
    flight[-1].wait()
    for h in range(2):
        def turned(ref, y):
            return [ref[pl.ds(h * 1600 + k * 8 + y, 8, 200), :] for k in range(25)]

        g = None
        for y in range(SY):
            d = [sd[pl.ds(h * 320 + a * 8 + y, 8, 40), :] for a in range(5)]
            for a in range(5):
                dturn[y, a, pl.ds(h * 8, 8), :] = d[a]
            g = d if g is None else sub(d, act(turned(ly, y), g))
            for a in range(5):
                gt[y, a] = g[a]
        for a in range(5):
            vec[a, pl.ds(h * 8, 8), :] = g[a]
        b = g
        for y in range(SY - 2, -1, -1):
            b = sub([gt[y, a] for a in range(5)], act(turned(uy, y), b))
        for a in range(5):
            vec[5 + a, pl.ds(h * 8, 8), :] = b[a]


def finish_kernel(z_ref, v1, v2, v3, m1, m2, m3, dturn, ly, uy, adjoint, metric, target,
                  spread, new, part, fin, sin, ft, ut, pk):
    z = z_ref[0]
    halves = [pl.ds(0, 8), pl.ds(8, 8)]
    zero = jnp.zeros((8, NN), jnp.float32)

    def a_of(v, h):
        return [v[j, halves[h], :] for j in range(5)]

    def b_of(v, h):
        return [v[5 + j, halves[h], :] for j in range(5)]

    def mat(m, at, h):
        return [m[25 * at + k, halves[h], :] for k in range(25)]

    def put_in(h, f):
        for j in range(5):
            fin[j, halves[h], :] = f[j]

    for h in range(2):
        @pl.when(z == 0)
        def _():
            put_in(h, [zero] * 5)

        @pl.when(z == 1)
        def _():
            put_in(h, a_of(v3, h))

        @pl.when(z == 2)
        def _():
            put_in(h, add(a_of(v3, h), act(mat(m3, 0, h), a_of(v2, h))))

        @pl.when(z == 3)
        def _():
            f = add(a_of(v2, h), act(mat(m2, 0, h), a_of(v1, h)))
            put_in(h, add(a_of(v3, h), act(mat(m3, 0, h), f)))

    def turned(ref, y, h):
        return [ref[pl.ds(h * 1600 + k * 8 + y, 8, 200), :] for k in range(25)]

    for h in range(2):
        f = [fin[j, halves[h], :] for j in range(5)]
        for y in range(SY):
            f = sub([dturn[y, a, halves[h], :] for a in range(5)], act(turned(ly, y, h), f))
            for a in range(5):
                ft[y, a, halves[h], :] = f[a]

    def put_back(h, s):
        for j in range(5):
            sin[j, halves[h], :] = s[j]

    for h in range(2):
        def own(h=h):
            return [ft[SY - 1, a, halves[h], :] for a in range(5)]

        @pl.when(z == 0)
        def _():
            f1 = own()
            f2 = add(a_of(v1, h), act(mat(m1, 0, h), f1))
            f3 = add(a_of(v2, h), act(mat(m2, 0, h), f2))
            s3 = add(b_of(v3, h), act(mat(m3, 0, h), f3))
            s2 = add(add(b_of(v2, h), act(mat(m2, 2, h), f2)), act(mat(m2, 1, h), s3))
            put_back(h, add(add(b_of(v1, h), act(mat(m1, 2, h), f1)), act(mat(m1, 1, h), s2)))

        @pl.when(z == 1)
        def _():
            f2 = own()
            f3 = add(a_of(v1, h), act(mat(m1, 0, h), f2))
            s3 = add(b_of(v2, h), act(mat(m2, 2, h), f3))
            put_back(h, add(add(b_of(v1, h), act(mat(m1, 2, h), f2)), act(mat(m1, 1, h), s3)))

        @pl.when(z == 2)
        def _():
            put_back(h, add(b_of(v1, h), act(mat(m1, 2, h), own())))

        @pl.when(z == 3)
        def _():
            put_back(h, [zero] * 5)

    for h in range(2):
        s = [sin[j, halves[h], :] for j in range(5)]
        for y in range(SY - 1, -1, -1):
            s = sub([ft[y, a, halves[h], :] for a in range(5)], act(turned(uy, y, h), s))
            for a in range(5):
                ut[pl.ds((y * 5 + a) * 16 + h * 8, 8), :] = s[a]

    for x in range(SX):
        fresh = []
        for a in range(5):
            fresh.append(adjoint[x, a] + ut[pl.ds(a * 16 + x, 8, 80), :])
            new[x, a] = fresh[a]
        for k in range(3):
            t = metric[x, 5 * k].astype(jnp.float32) * fresh[0]
            for a in range(1, 5):
                t = t + metric[x, 5 * k + a].astype(jnp.float32) * fresh[a]
            pk[k, pl.ds(x * 8, 8), :] = t

    group = lax.shift_right_logical(lax.broadcasted_iota(jnp.int32, (128, 128), 1), 4)
    value = jnp.zeros((128, 128), jnp.float32)
    for k in range(3):
        value = jnp.where(group % 3 == k, jnp.sum(pk[k], axis=1, keepdims=True), value)
    value = value * spread[...]
    high = value.astype(jnp.bfloat16).astype(jnp.float32)
    value = jnp.where(group < 3, high, value - high).astype(jnp.bfloat16)
    part[...] = jnp.dot(target[...].astype(jnp.bfloat16), value, preferred_element_type=jnp.float32)


def sum_kernel(parts, out):
    total = jnp.sum(parts[...], axis=0, keepdims=True)
    total = total + pltpu.roll(total, 80, 1)
    for k in range(3):
        part = total if k == 0 else pltpu.roll(total, 128 - 16 * k, 1)
        out[k : k + 1, :] = part[:, :16]


def call(kernel, outs, scratch, smem=0, vmem=0, hbm=0, sems=(), cost=0, limit=16):
    spec = pl.BlockSpec
    out_specs = [spec(memory_space=pltpu.HBM if isinstance(s, list) else pltpu.VMEM) for s in outs]
    return pl.pallas_call(
        kernel,
        out_shape=[pltpu.HBM(tuple(s), jnp.float32) if isinstance(s, list) else jax.ShapeDtypeStruct(s, jnp.float32)
                   for s in outs],
        in_specs=[spec(memory_space=pltpu.SMEM)] * smem + [spec(memory_space=pltpu.VMEM)] * vmem
        + [spec(memory_space=pltpu.HBM)] * hbm,
        out_specs=out_specs,
        scratch_shapes=[pltpu.VMEM(s, jnp.float32) for s in scratch]
        + [pltpu.SemaphoreType.DMA((n,)) for n in sems],
        compiler_params=pltpu.CompilerParams(vmem_limit_bytes=limit * 1024 * 1024),
        cost_estimate=pl.CostEstimate(flops=cost, bytes_accessed=cost, transcendentals=0),
    )


def in_hbm(x):
    return pltpu.with_memory_space_constraint(x, pltpu.HBM)


def shards(rhs, adjoint, diag_x, lower_x, upper_x, diag_y, lower_y, upper_y, metric, node_cell,
           node_owner, node_weight, node_count):
    def blocks(m):
        return m.transpose(0, 2, 3, 1, 4).reshape(SX, -1, SY, NN)

    rhs = rhs.transpose(0, 2, 1, 3)
    adjoint = adjoint.transpose(0, 2, 1, 3)
    dx, lx, ux, dy = blocks(diag_x), blocks(lower_x), blocks(upper_x), blocks(diag_y)
    ly = blocks(lower_y).reshape(-1, NN)
    uy = blocks(upper_y).reshape(-1, NN)
    metric = blocks(metric)
    z = lax.axis_index("span").astype(jnp.int32).reshape(1)

    tile, cells, msg_shape = (SX, 25, SY, NN), (SX, 5, SY, NN), (XS * ROWS, NN)
    msg, driven = call(
        stream_kernel,
        [msg_shape, list(cells)],
        [tile, tile, cells, tile, tile, cells, cells], hbm=4, sems=(14,), cost=10_000_000,
    )(in_hbm(rhs), in_hbm(dx), in_hbm(lx), in_hbm(ux))
    got = lax.all_to_all(msg.reshape(XS, ROWS, NN), "stream", 0, 0, tiled=True)
    (mats,) = call(
        span_kernel, [(75, SX, NN)], [(2 * SY, 25, 8, NN), uy.shape], vmem=1, hbm=2, sems=(1,), cost=10_000_000,
    )(ly, in_hbm(uy), in_hbm(driven))
    m1 = lax.ppermute(mats, "span", [(1, 0), (2, 1), (3, 2)])
    m2 = lax.ppermute(mats, "span", [(2, 0), (3, 1), (1, 3)])
    back, matsel = call(
        solve_kernel, [(XS, 8, NN), (25, SX, NN)],
        [(4, XS, ROWS, NN), (XS, 8, NN), (XS, 8, NN)], smem=1, vmem=1, hbm=1, sems=(1,), cost=10_000_000,
    )(z, got, in_hbm(mats))
    m3 = lax.ppermute(matsel, "span", [(3, 0), (1, 2), (2, 3)])
    back = lax.all_to_all(back, "stream", 0, 0, tiled=True)
    dturn, vec, target, spread, uy = call(
        replay_kernel,
        [(SY, 5, SX, NN), (10, SX, NN), (128, 128), (128, 128), uy.shape],
        [cells, tile, tile, tile, cells, (SX * 5 * SY, NN), (SY, 5, 8, NN)],
        smem=1, vmem=5, hbm=5, sems=(17,), cost=30_000_000,
    )(node_count.reshape(1), back.reshape(XS * 8, NN), node_cell.reshape(1, -1), node_owner.reshape(1, -1),
      node_weight.reshape(1, -1), ly, in_hbm(driven), in_hbm(lx), in_hbm(ux), in_hbm(dy), in_hbm(uy))
    v = [lax.ppermute(vec, "span", [((i + s) % 4, i) for i in range(4)]) for s in (1, 2, 3)]
    new, part = call(
        finish_kernel,
        [cells, (128, NN)],
        [(5, SX, NN), (5, SX, NN), (SY, 5, SX, NN), (SY * 5 * SX, NN), (3, 128, NN)],
        smem=1, vmem=13, cost=1_000_000,
    )(z, *v, m1, m2, m3, dturn, ly, uy, adjoint, metric, target, spread)
    parts = lax.all_to_all(part, ("stream", "span"), 0, 0, tiled=True)
    (control,) = call(sum_kernel, [(3, 16)], [], vmem=1)(parts)
    return new.transpose(0, 2, 1, 3), control


def solution(mesh):
    cells, mats = P("stream", "span", None, None), P("stream", "span", None, None, None)
    slots = P("stream", "span", None)
    return jax.shard_map(
        shards,
        mesh=mesh,
        in_specs=(cells,) * 2 + (mats,) * 7 + (slots,) * 3 + (P("stream", "span"),),
        out_specs=(cells, P(None, ("stream", "span"))),
        check_vma=False,
    )
```

```python
import jax
import jax.numpy as jnp
from jax import lax
from jax.experimental import pallas as pl
from jax.experimental.pallas import tpu as pltpu
from jax.sharding import PartitionSpec as P

SX, SY, NN = 16, 8, 128
XS = 32
ROWS = 24


def act(m, v):
    out = []
    for a in range(5):
        t = m[5 * a] * v[0]
        for b in range(1, 5):
            t = t + m[5 * a + b] * v[b]
        out.append(t)
    return out


def act_cols(m, f):
    cols = [act(m, [f[5 * b + c] for b in range(5)]) for c in range(5)]
    return [cols[c][a] for a in range(5) for c in range(5)]


def add(p, q):
    return [x + y for x, y in zip(p, q)]


def sub(p, q):
    return [x - y for x, y in zip(p, q)]


def lanes_quarter(shape):
    return lax.shift_right_logical(lax.broadcasted_iota(jnp.int32, shape, 1), 5)


def tiles(ref, i, n=25):
    return [ref[i, k] for k in range(n)]


def put(ref, i, vals):
    for k, v in enumerate(vals):
        ref[i, k] = v


def copies(pairs, sems):
    out = [pltpu.make_async_copy(src, dst, sems.at[k]) for k, (src, dst) in enumerate(pairs)]
    for c in out:
        c.start()
    return out


STEP = 4


def stream_kernel(rhs_h, dx_h, lx_h, ux_h, msg, driven_h, lx, ux, rhs, dx, fs, gs, driven, sems):
    chunks = [pl.ds(k * STEP, STEP) for k in range(SX // STEP)]
    pairs = []
    for c in chunks:
        pairs += [(lx_h.at[c], lx.at[c]), (dx_h.at[c], dx.at[c]), (rhs_h.at[c], rhs.at[c])]
    flight = copies(pairs + [(ux_h, ux)], sems)

    def fore(i, carry):
        g, f = carry
        l = tiles(lx, i)
        d = act(tiles(dx, i), tiles(rhs, i, 5))
        put(driven, i, d)
        g = sub(d, act(l, g))
        put(gs, i, g)
        f = act_cols(l, f)
        put(fs, i, f)
        return g, f

    for k in range(len(chunks)):
        for c in flight[3 * k : 3 * k + 3]:
            c.wait()
        if k == 0:
            g = act(tiles(dx, 0), tiles(rhs, 0, 5))
            put(driven, 0, g)
            put(gs, 0, g)
            f = tiles(lx, 0)
            put(fs, 0, f)
        g, f = lax.fori_loop(max(1, STEP * k), STEP * k + STEP, fore, (g, f), unroll=True)
    kept = pltpu.make_async_copy(driven, driven_h, sems.at[13])
    kept.start()
    flight[-1].wait()

    def back(k, carry):
        i = SX - 2 - k
        b, c = carry
        u = tiles(ux, i)
        b = sub(tiles(gs, i, 5), act(u, b))
        c = add(tiles(fs, i), act_cols(u, c))
        return b, c

    b, c = lax.fori_loop(0, SX - 1, back, (g, f), unroll=3)

    def back_map(k, bm):
        return act_cols(tiles(ux, SX - 2 - k), bm)

    bm = lax.fori_loop(0, SX - 1, back_map, tiles(ux, SX - 1), unroll=3)
    zero = jnp.zeros((SY, NN), jnp.float32)
    values = f + g + bm + b + [-x for x in c] + [zero] * 3
    quarter = lanes_quarter((SY, NN))
    for r in range(22):
        four = values[4 * r : 4 * r + 4]
        for nq in range(4):
            out = None
            for kk in range(4):
                shift = (32 * (kk - nq)) % 128
                part = four[kk] if shift == 0 else pltpu.roll(four[kk], shift, 1)
                out = part if out is None else jnp.where(quarter == kk, part, out)
            msg[pl.ds(nq * 8 * ROWS + r, 8, ROWS), :] = out
    for r in range(22, ROWS):
        for nq in range(4):
            msg[pl.ds(nq * 8 * ROWS + r, 8, ROWS), :] = zero
    kept.wait()


def span_kernel(ly, uy_h, after, mats, fy, uy, sems):
    del after
    (flight,) = copies([(uy_h, uy)], sems)
    def turned(ref, h, y):
        return [ref[pl.ds(h * 1600 + k * 8 + y, 8, 200), :] for k in range(25)]

    for h in range(2):
        f = turned(ly, h, 0)
        put(fy, 8 * h, f)

        def fore_y(y, f):
            f = act_cols(turned(ly, h, y), f)
            put(fy, 8 * h + y, f)
            return f

        f = lax.fori_loop(1, SY, fore_y, f, unroll=True)
        for k in range(25):
            mats[k, pl.ds(h * 8, 8), :] = f[k]
    flight.wait()
    for h in range(2):
        def back_y(k, c):
            y = SY - 2 - k
            return add(tiles(fy, 8 * h + y), act_cols(turned(uy, h, y), c))

        c = lax.fori_loop(0, SY - 1, back_y, tiles(fy, 8 * h + SY - 1), unroll=True)
        for k in range(25):
            mats[50 + k, pl.ds(h * 8, 8), :] = -c[k]

        def back_map_y(k, bm):
            return act_cols(turned(uy, h, SY - 2 - k), bm)

        bm = lax.fori_loop(0, SY - 1, back_map_y, turned(uy, h, SY - 1), unroll=True)
        for k in range(25):
            mats[25 + k, pl.ds(h * 8, 8), :] = bm[k]


def solve_kernel(got, out, un, fin, sin):
    un[0] = got[...]
    for q in range(1, 4):
        for p in range(XS):
            un[q, p] = pltpu.roll(got[p], 128 - 32 * q, 1)

    def val(p, k):
        return un[k % 4, p, (k // 4) : (k // 4) + 1, :]

    zero = [jnp.zeros((1, NN), jnp.float32)] * 5

    def fore(p, f):
        for j in range(5):
            fin[p, j : j + 1, :] = f[j]
        return add(act([val(p, k) for k in range(25)], f), [val(p, 25 + j) for j in range(5)])

    lax.fori_loop(0, XS, fore, zero, unroll=8)

    def back(k, s):
        p = XS - 1 - k
        for j in range(5):
            sin[p, j : j + 1, :] = s[j]
        f = [fin[p, j : j + 1, :] for j in range(5)]
        known = add(act([val(p, 60 + k) for k in range(25)], f), [val(p, 55 + j) for j in range(5)])
        return add(known, act([val(p, 30 + k) for k in range(25)], s))

    lax.fori_loop(0, XS, back, zero, unroll=8)
    quarter = lanes_quarter((8, NN))
    for p in range(XS):
        out[p] = jnp.where(quarter == 0, fin[p], pltpu.roll(sin[p], 32, 1))


def replay_kernel(count, got, cell, owner, weight, ly, driven_h, lx_h, ux_h, dy_h, uy_h, dturn, vec, target,
                  spread, uy, driven, lx, ux, dy, fs, sd, gt, sems):
    chunks = [pl.ds(k * STEP, STEP) for k in range(SX // STEP)]
    pairs = []
    for c in chunks:
        pairs += [(lx_h.at[c], lx.at[c]), (driven_h.at[c], driven.at[c])]
    for c in chunks[::-1]:
        pairs += [(ux_h.at[c], ux.at[c]), (dy_h.at[c], dy.at[c])]
    flight = copies(pairs + [(uy_h, uy)], sems)

    row = lax.broadcasted_iota(jnp.int32, (128, 128), 0)
    lane = lax.broadcasted_iota(jnp.int32, (128, 128), 1)
    here = cell[...] == row
    used = jnp.logical_and(here, lane < count[0])
    w = jnp.sum(jnp.where(used, weight[...], 0.0), axis=1, keepdims=True)
    who = jnp.sum(jnp.where(here, owner[...].astype(jnp.float32), 0.0), axis=1, keepdims=True)
    who = who.astype(jnp.int32)
    target[...] = (lax.shift_right_logical(who, 4) == lane).astype(jnp.float32).T
    mine = jnp.logical_and(lane < 96, (lane & 15) == (who & 15))
    spread[...] = jnp.where(mine, w, 0.0)


    quarter = lanes_quarter((SY, NN))

    def entering(j, at):
        out = None
        for nq in range(4):
            part = got[pl.ds(nq * 64 + j, 8, 8), :]
            shift = (32 * nq - 32 * at) % 128
            part = part if shift == 0 else pltpu.roll(part, shift, 1)
            out = part if out is None else jnp.where(quarter == nq, part, out)
        return out

    def fore(i, f):
        f = sub(tiles(driven, i, 5), act(tiles(lx, i), f))
        for a in range(5):
            fs[i, a] = f[a]
        return f

    f = [entering(j, 0) for j in range(5)]
    for k in range(len(chunks)):
        for c in flight[2 * k : 2 * k + 2]:
            c.wait()
        f = lax.fori_loop(STEP * k, STEP * k + STEP, fore, f)

    def back(k, s):
        i = SX - 1 - k
        s = sub(tiles(fs, i, 5), act(tiles(ux, i), s))
        d = act(tiles(dy, i), s)
        for a in range(5):
            sd[pl.ds(pl.multiple_of((i * 5 + a) * 8, 8), 8), :] = d[a]
        return s

    s = [entering(j, 1) for j in range(5)]
    for k in range(len(chunks)):
        for c in flight[2 * len(chunks) + 2 * k : 2 * len(chunks) + 2 * k + 2]:
            c.wait()
        s = lax.fori_loop(STEP * k, STEP * k + STEP, back, s)
    flight[-1].wait()
    for h in range(2):
        def turned(ref, y):
            return [ref[pl.ds(h * 1600 + k * 8 + y, 8, 200), :] for k in range(25)]

        g = None
        for y in range(SY):
            d = [sd[pl.ds(h * 320 + a * 8 + y, 8, 40), :] for a in range(5)]
            for a in range(5):
                dturn[y, a, pl.ds(h * 8, 8), :] = d[a]
            g = d if g is None else sub(d, act(turned(ly, y), g))
            for a in range(5):
                gt[y, a] = g[a]
        for a in range(5):
            vec[a, pl.ds(h * 8, 8), :] = g[a]
        b = g
        for y in range(SY - 2, -1, -1):
            b = sub([gt[y, a] for a in range(5)], act(turned(uy, y), b))
        for a in range(5):
            vec[5 + a, pl.ds(h * 8, 8), :] = b[a]


HALVES = [pl.ds(0, 8), pl.ds(8, 8)]


def part_of(v, at, h, n=5):
    return [v[at + k, HALVES[h], :] for k in range(n)]


def by_side(z_ref, body):
    @pl.when((z_ref[0] & 1) == 0)
    def _():
        body(0, 1)

    @pl.when((z_ref[0] & 1) == 1)
    def _():
        body(1, 0)


def pair_kernel(z_ref, mats, other, out):
    m = [mats, other]

    def body(lo, up):
        for h in range(2):
            t = act_cols(part_of(m[up], 50, h, 25), part_of(m[lo], 0, h, 25))
            t = add(part_of(m[lo], 50, h, 25), act_cols(part_of(m[lo], 25, h, 25), t))
            for k in range(25):
                out[k, HALVES[h], :] = t[k]

    by_side(z_ref, body)


def join_kernel(z_ref, vec, near, mats, other, out):
    m, v = [mats, other], [vec, near]

    def body(lo, up):
        def put_out(h, t):
            for j in range(5):
                out[j, HALVES[h], :] = t[j]

        for h in range(2):
            @pl.when(z_ref[0] < 2)
            def _():
                put_out(h, add(part_of(v[up], 0, h), act(part_of(m[up], 0, h, 25), part_of(v[lo], 0, h))))

            @pl.when(z_ref[0] >= 2)
            def _():
                t = add(part_of(v[up], 5, h), act(part_of(m[up], 50, h, 25), part_of(v[lo], 0, h)))
                put_out(h, add(part_of(v[lo], 5, h), act(part_of(m[lo], 25, h, 25), t)))

    by_side(z_ref, body)


def finish_kernel(z_ref, vec, near, beyond, mats, other, far, dturn, ly, uy, adjoint, metric, target,
                  spread, new, part, fin, sin, ft, ut, pk):
    z = z_ref[0]
    halves = HALVES
    zero = [jnp.zeros((8, NN), jnp.float32)] * 5

    def put_in(h, f):
        for j in range(5):
            fin[j, halves[h], :] = f[j]

    def put_back(h, s):
        for j in range(5):
            sin[j, halves[h], :] = s[j]

    for h in range(2):
        def lower(m1, a0, a1):
            f2 = add(a1, act(part_of(m1, 0, h, 25), a0))
            return add(part_of(beyond, 0, h), act(part_of(far, 0, h, 25), f2))

        @pl.when(z == 0)
        def _():
            put_in(h, zero)
            a0 = part_of(vec, 0, h)
            s2 = lower(other, a0, part_of(near, 0, h))
            s1 = add(part_of(near, 5, h), act(part_of(other, 50, h, 25), a0))
            put_back(h, add(s1, act(part_of(other, 25, h, 25), s2)))

        @pl.when(z == 1)
        def _():
            a0 = part_of(near, 0, h)
            put_in(h, a0)
            put_back(h, lower(mats, a0, part_of(vec, 0, h)))

        @pl.when(z == 2)
        def _():
            f2 = part_of(beyond, 0, h)
            put_in(h, f2)
            f3 = add(part_of(vec, 0, h), act(part_of(mats, 0, h, 25), f2))
            put_back(h, add(part_of(near, 5, h), act(part_of(other, 50, h, 25), f3)))

        @pl.when(z == 3)
        def _():
            put_in(h, add(part_of(near, 0, h), act(part_of(other, 0, h, 25), part_of(beyond, 0, h))))
            put_back(h, zero)

    def turned(ref, y, h):
        return [ref[pl.ds(h * 1600 + k * 8 + y, 8, 200), :] for k in range(25)]

    for h in range(2):
        f = [fin[j, halves[h], :] for j in range(5)]
        for y in range(SY):
            f = sub([dturn[y, a, halves[h], :] for a in range(5)], act(turned(ly, y, h), f))
            for a in range(5):
                ft[y, a, halves[h], :] = f[a]

    for h in range(2):
        s = [sin[j, halves[h], :] for j in range(5)]
        for y in range(SY - 1, -1, -1):
            s = sub([ft[y, a, halves[h], :] for a in range(5)], act(turned(uy, y, h), s))
            for a in range(5):
                ut[pl.ds((y * 5 + a) * 16 + h * 8, 8), :] = s[a]

    for x in range(SX):
        fresh = []
        for a in range(5):
            fresh.append(adjoint[x, a] + ut[pl.ds(a * 16 + x, 8, 80), :])
            new[x, a] = fresh[a]
        for k in range(3):
            t = metric[x, 5 * k].astype(jnp.float32) * fresh[0]
            for a in range(1, 5):
                t = t + metric[x, 5 * k + a].astype(jnp.float32) * fresh[a]
            pk[k, pl.ds(x * 8, 8), :] = t

    group = lax.shift_right_logical(lax.broadcasted_iota(jnp.int32, (128, 128), 1), 4)
    value = jnp.zeros((128, 128), jnp.float32)
    for k in range(3):
        value = jnp.where(group % 3 == k, jnp.sum(pk[k], axis=1, keepdims=True), value)
    value = value * spread[...]
    high = value.astype(jnp.bfloat16).astype(jnp.float32)
    value = jnp.where(group < 3, high, value - high).astype(jnp.bfloat16)
    part[...] = jnp.dot(target[...].astype(jnp.bfloat16), value, preferred_element_type=jnp.float32)


def sum_kernel(parts, out):
    total = jnp.sum(parts[...], axis=0, keepdims=True)
    total = total + pltpu.roll(total, 80, 1)
    for k in range(3):
        part = total if k == 0 else pltpu.roll(total, 128 - 16 * k, 1)
        out[k : k + 1, :] = part[:, :16]


def call(kernel, outs, scratch, smem=0, vmem=0, hbm=0, sems=(), cost=0, limit=16):
    spec = pl.BlockSpec
    out_specs = [spec(memory_space=pltpu.HBM if isinstance(s, list) else pltpu.VMEM) for s in outs]
    return pl.pallas_call(
        kernel,
        out_shape=[pltpu.HBM(tuple(s), jnp.float32) if isinstance(s, list) else jax.ShapeDtypeStruct(s, jnp.float32)
                   for s in outs],
        in_specs=[spec(memory_space=pltpu.SMEM)] * smem + [spec(memory_space=pltpu.VMEM)] * vmem
        + [spec(memory_space=pltpu.HBM)] * hbm,
        out_specs=out_specs,
        scratch_shapes=[pltpu.VMEM(s, jnp.float32) for s in scratch]
        + [pltpu.SemaphoreType.DMA((n,)) for n in sems],
        compiler_params=pltpu.CompilerParams(vmem_limit_bytes=limit * 1024 * 1024),
        cost_estimate=pl.CostEstimate(flops=int(cost * 1e9), bytes_accessed=1000, transcendentals=0),
    )


def in_hbm(x):
    return pltpu.with_memory_space_constraint(x, pltpu.HBM)


def shards(rhs, adjoint, diag_x, lower_x, upper_x, diag_y, lower_y, upper_y, metric, node_cell,
           node_owner, node_weight, node_count):
    def blocks(m):
        return m.transpose(0, 2, 3, 1, 4).reshape(SX, -1, SY, NN)

    rhs = rhs.transpose(0, 2, 1, 3)
    adjoint = adjoint.transpose(0, 2, 1, 3)
    dx, lx, ux, dy = blocks(diag_x), blocks(lower_x), blocks(upper_x), blocks(diag_y)
    ly = blocks(lower_y).reshape(-1, NN)
    uy = blocks(upper_y).reshape(-1, NN)
    metric = blocks(metric)
    z = lax.axis_index("span").astype(jnp.int32).reshape(1)

    tile, cells, msg_shape = (SX, 25, SY, NN), (SX, 5, SY, NN), (XS * ROWS, NN)
    msg, driven = call(
        stream_kernel,
        [msg_shape, list(cells)],
        [tile, tile, cells, tile, tile, cells, cells], hbm=4, sems=(14,), cost=4,
    )(in_hbm(rhs), in_hbm(dx), in_hbm(lx), in_hbm(ux))
    got = lax.all_to_all(msg.reshape(XS, ROWS, NN), "stream", 0, 0, tiled=True)
    (mats,) = call(
        span_kernel, [(75, SX, NN)], [(2 * SY, 25, 8, NN), uy.shape], vmem=1, hbm=2, sems=(1,), cost=3,
    )(ly, in_hbm(uy), in_hbm(driven))
    other = lax.ppermute(mats, "span", [(1, 0), (2, 3), (3, 2)])
    (back,) = call(
        solve_kernel, [(XS, 8, NN)],
        [(4, XS, ROWS, NN), (XS, 8, NN), (XS, 8, NN)], vmem=1, cost=12,
    )(got)
    (pair,) = call(pair_kernel, [(25, SX, NN)], [], smem=1, vmem=2, cost=0.2)(z, mats, other)
    far = lax.ppermute(pair, "span", [(2, 0), (3, 1)])
    back = lax.all_to_all(back, "stream", 0, 0, tiled=True)
    dturn, vec, target, spread, uy = call(
        replay_kernel,
        [(SY, 5, SX, NN), (10, SX, NN), (128, 128), (128, 128), uy.shape],
        [cells, tile, tile, tile, cells, (SX * 5 * SY, NN), (SY, 5, 8, NN)],
        smem=1, vmem=5, hbm=5, sems=(17,), cost=4,
    )(node_count.reshape(1), back.reshape(XS * 8, NN), node_cell.reshape(1, -1), node_owner.reshape(1, -1),
      node_weight.reshape(1, -1), ly, in_hbm(driven), in_hbm(lx), in_hbm(ux), in_hbm(dy), in_hbm(uy))
    near = lax.ppermute(vec, "span", [(i, i ^ 1) for i in range(4)])
    (joint,) = call(join_kernel, [(5, SX, NN)], [], smem=1, vmem=4, cost=0.1)(z, vec, near, mats, other)
    beyond = lax.ppermute(joint, "span", [(i, i ^ 2) for i in range(4)])
    new, part = call(
        finish_kernel,
        [cells, (128, NN)],
        [(5, SX, NN), (5, SX, NN), (SY, 5, SX, NN), (SY * 5 * SX, NN), (3, 128, NN)],
        smem=1, vmem=13, cost=2,
    )(z, vec, near, beyond, mats, other, far, dturn, ly, uy, adjoint, metric, target, spread)
    parts = lax.all_to_all(part, ("stream", "span"), 0, 0, tiled=True)
    (control,) = call(sum_kernel, [(3, 16)], [], vmem=1)(parts)
    return new.transpose(0, 2, 1, 3), control


def solution(mesh):
    cells, mats = P("stream", "span", None, None), P("stream", "span", None, None, None)
    slots = P("stream", "span", None)
    return jax.shard_map(
        shards,
        mesh=mesh,
        in_specs=(cells,) * 2 + (mats,) * 7 + (slots,) * 3 + (P("stream", "span"),),
        out_specs=(cells, P(None, ("stream", "span"))),
        check_vma=False,
    )
```

```python
import jax
import jax.numpy as jnp
from jax import lax
from jax.experimental import pallas as pl
from jax.experimental.pallas import tpu as pltpu
from jax.sharding import PartitionSpec as P

SX, SY, NN = 16, 8, 128
XS = 32
ROWS = 24


def act(m, v):
    out = []
    for a in range(5):
        t = m[5 * a] * v[0]
        for b in range(1, 5):
            t = t + m[5 * a + b] * v[b]
        out.append(t)
    return out


def act_cols(m, f):
    cols = [act(m, [f[5 * b + c] for b in range(5)]) for c in range(5)]
    return [cols[c][a] for a in range(5) for c in range(5)]


def add(p, q):
    return [x + y for x, y in zip(p, q)]


def sub(p, q):
    return [x - y for x, y in zip(p, q)]


def lanes_quarter(shape):
    return lax.shift_right_logical(lax.broadcasted_iota(jnp.int32, shape, 1), 5)


def tiles(ref, i, n=25):
    return [ref[i, k] for k in range(n)]


def put(ref, i, vals):
    for k, v in enumerate(vals):
        ref[i, k] = v


def copies(pairs, sems):
    out = [pltpu.make_async_copy(src, dst, sems.at[k]) for k, (src, dst) in enumerate(pairs)]
    for c in out:
        c.start()
    return out


STEP = 4


def maps_kernel(rhs_h, dx_h, lx_h, ux_h, ly_h, uy_h, msg_h, driven_h, mats,
                lx, ux, rhs, dx, fs, gs, driven, msg, ly, uy, fy, sems):
    chunks = [pl.ds(k * STEP, STEP) for k in range(SX // STEP)]
    halves = [pl.ds(SX // 2, SX // 2), pl.ds(0, SX // 2)]
    pairs = [(ux_h.at[c], ux.at[c]) for c in halves]
    pairs += [(rhs_h, rhs)]
    for c in chunks:
        pairs += [(lx_h.at[c], lx.at[c]), (dx_h.at[c], dx.at[c])]
    late = len(pairs)
    pairs += [(ly_h, ly), (uy_h, uy)]
    flight = copies(pairs, sems)
    out_sem = len(pairs)

    def back_map(k, bm):
        return act_cols(tiles(ux, SX - 2 - k), bm)

    flight[0].wait()
    bm = lax.fori_loop(0, SX // 2 - 1, back_map, tiles(ux, SX - 1), unroll=True)
    flight[1].wait()
    bm = lax.fori_loop(SX // 2 - 1, SX - 1, back_map, bm, unroll=True)

    def fore(i, carry):
        g, f = carry
        l = tiles(lx, i)
        d = act(tiles(dx, i), tiles(rhs, i, 5))
        put(driven, i, d)
        g = sub(d, act(l, g))
        put(gs, i, g)
        f = act_cols(l, f)
        put(fs, i, f)
        return g, f

    for k in range(len(chunks)):
        for c in flight[3 + 2 * k : 5 + 2 * k]:
            c.wait()
        if k == 0:
            flight[2].wait()
            g = act(tiles(dx, 0), tiles(rhs, 0, 5))
            put(driven, 0, g)
            put(gs, 0, g)
            f = tiles(lx, 0)
            put(fs, 0, f)
        g, f = lax.fori_loop(max(1, STEP * k), STEP * k + STEP, fore, (g, f), unroll=True)
    kept = pltpu.make_async_copy(driven, driven_h, sems.at[out_sem])
    kept.start()

    def back(k, carry):
        i = SX - 2 - k
        b, c = carry
        u = tiles(ux, i)
        b = sub(tiles(gs, i, 5), act(u, b))
        c = add(tiles(fs, i), act_cols(u, c))
        return b, c

    b, c = lax.fori_loop(0, SX - 1, back, (g, f), unroll=3)
    zero = jnp.zeros((SY, NN), jnp.float32)
    values = f + g + bm + b + [-x for x in c] + [zero] * 3
    quarter = lanes_quarter((SY, NN))
    for r in range(22):
        four = values[4 * r : 4 * r + 4]
        for nq in range(4):
            out = None
            for kk in range(4):
                shift = (32 * (kk - nq)) % 128
                part = four[kk] if shift == 0 else pltpu.roll(four[kk], shift, 1)
                out = part if out is None else jnp.where(quarter == kk, part, out)
            msg[pl.ds(nq * 8 * ROWS + r, 8, ROWS), :] = out
    for r in range(22, ROWS):
        for nq in range(4):
            msg[pl.ds(nq * 8 * ROWS + r, 8, ROWS), :] = zero
    sent = pltpu.make_async_copy(msg, msg_h, sems.at[out_sem + 1])
    sent.start()

    def turned(ref, h, y):
        return [ref[pl.ds(h * 1600 + k * 8 + y, 8, 200), :] for k in range(25)]

    flight[late].wait()
    for h in range(2):
        f = turned(ly, h, 0)
        put(fy, 8 * h, f)

        def fore_y(y, f):
            f = act_cols(turned(ly, h, y), f)
            put(fy, 8 * h + y, f)
            return f

        f = lax.fori_loop(1, SY, fore_y, f, unroll=True)
        for k in range(25):
            mats[k, pl.ds(h * 8, 8), :] = f[k]
    flight[late + 1].wait()
    for h in range(2):
        def back_y(k, c):
            y = SY - 2 - k
            return add(tiles(fy, 8 * h + y), act_cols(turned(uy, h, y), c))

        c = lax.fori_loop(0, SY - 1, back_y, tiles(fy, 8 * h + SY - 1), unroll=True)
        for k in range(25):
            mats[50 + k, pl.ds(h * 8, 8), :] = -c[k]

        def back_map_y(k, bm):
            return act_cols(turned(uy, h, SY - 2 - k), bm)

        bm = lax.fori_loop(0, SY - 1, back_map_y, turned(uy, h, SY - 1), unroll=True)
        for k in range(25):
            mats[25 + k, pl.ds(h * 8, 8), :] = bm[k]
    sent.wait()
    kept.wait()


def solve_kernel(got, out, un, fin, sin):
    un[0] = got[...]
    for q in range(1, 4):
        for p in range(XS):
            un[q, p] = pltpu.roll(got[p], 128 - 32 * q, 1)

    def val(p, k):
        return un[k % 4, p, (k // 4) : (k // 4) + 1, :]

    zero = [jnp.zeros((1, NN), jnp.float32)] * 5

    def fore(p, f):
        for j in range(5):
            fin[p, j : j + 1, :] = f[j]
        return add(act([val(p, k) for k in range(25)], f), [val(p, 25 + j) for j in range(5)])

    lax.fori_loop(0, XS, fore, zero, unroll=16)

    def back(k, s):
        p = XS - 1 - k
        for j in range(5):
            sin[p, j : j + 1, :] = s[j]
        f = [fin[p, j : j + 1, :] for j in range(5)]
        known = add(act([val(p, 60 + k) for k in range(25)], f), [val(p, 55 + j) for j in range(5)])
        return add(known, act([val(p, 30 + k) for k in range(25)], s))

    lax.fori_loop(0, XS, back, zero, unroll=16)
    quarter = lanes_quarter((8, NN))
    for p in range(XS):
        out[p] = jnp.where(quarter == 0, fin[p], pltpu.roll(sin[p], 32, 1))


def replay_kernel(count, got, cell, owner, weight, ly, driven_h, lx_h, ux_h, dy_h, uy_h, dturn, vec, target,
                  spread, uy, driven, lx, ux, dy, fs, sd, gt, sems):
    step = SX // 2
    halves = [pl.ds(0, step), pl.ds(step, step)]
    pairs = [(driven_h, driven)] + [(lx_h.at[c], lx.at[c]) for c in halves]
    for c in halves[::-1]:
        pairs += [(ux_h.at[c], ux.at[c]), (dy_h.at[c], dy.at[c])]
    flight = copies(pairs + [(uy_h, uy)], sems)

    row = lax.broadcasted_iota(jnp.int32, (128, 128), 0)
    lane = lax.broadcasted_iota(jnp.int32, (128, 128), 1)
    here = cell[...] == row
    used = jnp.logical_and(here, lane < count[0])
    w = jnp.sum(jnp.where(used, weight[...], 0.0), axis=1, keepdims=True)
    who = jnp.sum(jnp.where(here, owner[...].astype(jnp.float32), 0.0), axis=1, keepdims=True)
    who = who.astype(jnp.int32)
    target[...] = (lax.shift_right_logical(who, 4) == lane).astype(jnp.float32).T
    mine = jnp.logical_and(lane < 96, (lane & 15) == (who & 15))
    spread[...] = jnp.where(mine, w, 0.0)


    quarter = lanes_quarter((SY, NN))

    def entering(j, at):
        out = None
        for nq in range(4):
            part = got[pl.ds(nq * 64 + j, 8, 8), :]
            shift = (32 * nq - 32 * at) % 128
            part = part if shift == 0 else pltpu.roll(part, shift, 1)
            out = part if out is None else jnp.where(quarter == nq, part, out)
        return out

    def fore(i, f):
        f = sub(tiles(driven, i, 5), act(tiles(lx, i), f))
        for a in range(5):
            fs[i, a] = f[a]
        return f

    f = [entering(j, 0) for j in range(5)]
    flight[0].wait()
    for k in range(2):
        flight[1 + k].wait()
        f = lax.fori_loop(step * k, step * k + step, fore, f, unroll=2)

    def back(k, s):
        i = SX - 1 - k
        s = sub(tiles(fs, i, 5), act(tiles(ux, i), s))
        d = act(tiles(dy, i), s)
        for a in range(5):
            sd[pl.ds(pl.multiple_of((i * 5 + a) * 8, 8), 8), :] = d[a]
        return s

    s = [entering(j, 1) for j in range(5)]
    for k in range(2):
        flight[3 + 2 * k].wait()
        flight[4 + 2 * k].wait()
        s = lax.fori_loop(step * k, step * k + step, back, s, unroll=2)
    flight[-1].wait()
    for h in range(2):
        def turned(ref, y):
            return [ref[pl.ds(h * 1600 + k * 8 + y, 8, 200), :] for k in range(25)]

        g = None
        for y in range(SY):
            d = [sd[pl.ds(h * 320 + a * 8 + y, 8, 40), :] for a in range(5)]
            for a in range(5):
                dturn[y, a, pl.ds(h * 8, 8), :] = d[a]
            g = d if g is None else sub(d, act(turned(ly, y), g))
            for a in range(5):
                gt[y, a] = g[a]
        for a in range(5):
            vec[a, pl.ds(h * 8, 8), :] = g[a]
        b = g
        for y in range(SY - 2, -1, -1):
            b = sub([gt[y, a] for a in range(5)], act(turned(uy, y), b))
        for a in range(5):
            vec[5 + a, pl.ds(h * 8, 8), :] = b[a]


HALVES = [pl.ds(0, 8), pl.ds(8, 8)]


def part_of(v, at, h, n=5):
    return [v[at + k, HALVES[h], :] for k in range(n)]


def by_side(z_ref, body):
    @pl.when((z_ref[0] & 1) == 0)
    def _():
        body(0, 1)

    @pl.when((z_ref[0] & 1) == 1)
    def _():
        body(1, 0)


def pair_kernel(z_ref, mats, other, out):
    m = [mats, other]

    def body(lo, up):
        for h in range(2):
            t = act_cols(part_of(m[up], 50, h, 25), part_of(m[lo], 0, h, 25))
            t = add(part_of(m[lo], 50, h, 25), act_cols(part_of(m[lo], 25, h, 25), t))
            for k in range(25):
                out[k, HALVES[h], :] = t[k]

    by_side(z_ref, body)


def join_kernel(z_ref, vec, near, mats, other, out):
    m, v = [mats, other], [vec, near]

    def body(lo, up):
        def put_out(h, t):
            for j in range(5):
                out[j, HALVES[h], :] = t[j]

        for h in range(2):
            @pl.when(z_ref[0] < 2)
            def _():
                put_out(h, add(part_of(v[up], 0, h), act(part_of(m[up], 0, h, 25), part_of(v[lo], 0, h))))

            @pl.when(z_ref[0] >= 2)
            def _():
                t = add(part_of(v[up], 5, h), act(part_of(m[up], 50, h, 25), part_of(v[lo], 0, h)))
                put_out(h, add(part_of(v[lo], 5, h), act(part_of(m[lo], 25, h, 25), t)))

    by_side(z_ref, body)


def finish_kernel(z_ref, vec, near, beyond, mats, other, far, dturn, ly, uy, adjoint, metric, target,
                  spread, new_h, part, fin, sin, ft, ut, pk, new, sems):
    z = z_ref[0]
    halves = HALVES
    zero = [jnp.zeros((8, NN), jnp.float32)] * 5

    def put_in(h, f):
        for j in range(5):
            fin[j, halves[h], :] = f[j]

    def put_back(h, s):
        for j in range(5):
            sin[j, halves[h], :] = s[j]

    for h in range(2):
        def lower(m1, a0, a1):
            f2 = add(a1, act(part_of(m1, 0, h, 25), a0))
            return add(part_of(beyond, 0, h), act(part_of(far, 0, h, 25), f2))

        @pl.when(z == 0)
        def _():
            put_in(h, zero)
            a0 = part_of(vec, 0, h)
            s2 = lower(other, a0, part_of(near, 0, h))
            s1 = add(part_of(near, 5, h), act(part_of(other, 50, h, 25), a0))
            put_back(h, add(s1, act(part_of(other, 25, h, 25), s2)))

        @pl.when(z == 1)
        def _():
            a0 = part_of(near, 0, h)
            put_in(h, a0)
            put_back(h, lower(mats, a0, part_of(vec, 0, h)))

        @pl.when(z == 2)
        def _():
            f2 = part_of(beyond, 0, h)
            put_in(h, f2)
            f3 = add(part_of(vec, 0, h), act(part_of(mats, 0, h, 25), f2))
            put_back(h, add(part_of(near, 5, h), act(part_of(other, 50, h, 25), f3)))

        @pl.when(z == 3)
        def _():
            put_in(h, add(part_of(near, 0, h), act(part_of(other, 0, h, 25), part_of(beyond, 0, h))))
            put_back(h, zero)

    def turned(ref, y, h):
        return [ref[pl.ds(h * 1600 + k * 8 + y, 8, 200), :] for k in range(25)]

    for h in range(2):
        f = [fin[j, halves[h], :] for j in range(5)]
        for y in range(SY):
            f = sub([dturn[y, a, halves[h], :] for a in range(5)], act(turned(ly, y, h), f))
            for a in range(5):
                ft[y, a, halves[h], :] = f[a]

    for h in range(2):
        s = [sin[j, halves[h], :] for j in range(5)]
        for y in range(SY - 1, -1, -1):
            s = sub([ft[y, a, halves[h], :] for a in range(5)], act(turned(uy, y, h), s))
            for a in range(5):
                ut[pl.ds((y * 5 + a) * 16 + h * 8, 8), :] = s[a]

    for x in range(SX):
        for a in range(5):
            new[x, a] = adjoint[x, a] + ut[pl.ds(a * 16 + x, 8, 80), :]
    sent = pltpu.make_async_copy(new, new_h, sems.at[0])
    sent.start()
    for x in range(SX):
        fresh = tiles(new, x, 5)
        for k in range(3):
            t = metric[x, 5 * k].astype(jnp.float32) * fresh[0]
            for a in range(1, 5):
                t = t + metric[x, 5 * k + a].astype(jnp.float32) * fresh[a]
            pk[k, pl.ds(x * 8, 8), :] = t

    group = lax.shift_right_logical(lax.broadcasted_iota(jnp.int32, (128, 128), 1), 4)
    value = jnp.zeros((128, 128), jnp.float32)
    for k in range(3):
        value = jnp.where(group % 3 == k, jnp.sum(pk[k], axis=1, keepdims=True), value)
    value = value * spread[...]
    high = value.astype(jnp.bfloat16).astype(jnp.float32)
    value = jnp.where(group < 3, high, value - high).astype(jnp.bfloat16)
    part[...] = jnp.dot(target[...].astype(jnp.bfloat16), value, preferred_element_type=jnp.float32)
    sent.wait()


def sum_kernel(parts, out):
    total = jnp.sum(parts[...], axis=0, keepdims=True)
    total = total + pltpu.roll(total, 80, 1)
    for k in range(3):
        part = total if k == 0 else pltpu.roll(total, 128 - 16 * k, 1)
        out[k : k + 1, :] = part[:, :16]


def call(kernel, outs, scratch, smem=0, vmem=0, hbm=0, sems=(), cost=0, limit=16):
    spec = pl.BlockSpec
    out_specs = [spec(memory_space=pltpu.HBM if isinstance(s, list) else pltpu.VMEM) for s in outs]
    return pl.pallas_call(
        kernel,
        out_shape=[pltpu.HBM(tuple(s), jnp.float32) if isinstance(s, list) else jax.ShapeDtypeStruct(s, jnp.float32)
                   for s in outs],
        in_specs=[spec(memory_space=pltpu.SMEM)] * smem + [spec(memory_space=pltpu.VMEM)] * vmem
        + [spec(memory_space=pltpu.HBM)] * hbm,
        out_specs=out_specs,
        scratch_shapes=[pltpu.VMEM(s, jnp.float32) for s in scratch]
        + [pltpu.SemaphoreType.DMA((n,)) for n in sems],
        compiler_params=pltpu.CompilerParams(vmem_limit_bytes=limit * 1024 * 1024),
        cost_estimate=pl.CostEstimate(flops=int(cost * 1e9), bytes_accessed=1000, transcendentals=0),
    )


def in_hbm(x):
    return pltpu.with_memory_space_constraint(x, pltpu.HBM)


def shards(rhs, adjoint, diag_x, lower_x, upper_x, diag_y, lower_y, upper_y, metric, node_cell,
           node_owner, node_weight, node_count):
    def blocks(m):
        return m.transpose(0, 2, 3, 1, 4).reshape(SX, -1, SY, NN)

    rhs = rhs.transpose(0, 2, 1, 3)
    adjoint = adjoint.transpose(0, 2, 1, 3)
    dx, lx, ux, dy = blocks(diag_x), blocks(lower_x), blocks(upper_x), blocks(diag_y)
    ly = blocks(lower_y).reshape(-1, NN)
    uy = blocks(upper_y).reshape(-1, NN)
    metric = blocks(metric)
    z = lax.axis_index("span").astype(jnp.int32).reshape(1)

    tile, cells, msg_shape = (SX, 25, SY, NN), (SX, 5, SY, NN), (XS * ROWS, NN)
    msg, driven, mats = call(
        maps_kernel,
        [list(msg_shape), list(cells), (75, SX, NN)],
        [tile, tile, cells, tile, tile, cells, cells, msg_shape, ly.shape, uy.shape, (2 * SY, 25, 8, NN)],
        hbm=6, sems=(15,), cost=7, limit=20,
    )(in_hbm(rhs), in_hbm(dx), in_hbm(lx), in_hbm(ux), in_hbm(ly), in_hbm(uy))
    got = lax.all_to_all(msg.reshape(XS, ROWS, NN), "stream", 0, 0, tiled=True)
    other = lax.ppermute(mats, "span", [(1, 0), (2, 3), (3, 2)])
    (back,) = call(
        solve_kernel, [(XS, 8, NN)],
        [(4, XS, ROWS, NN), (XS, 8, NN), (XS, 8, NN)], vmem=1, cost=12,
    )(got)
    (pair,) = call(pair_kernel, [(25, SX, NN)], [], smem=1, vmem=2, cost=0.2)(z, mats, other)
    far = lax.ppermute(pair, "span", [(3, 0), (2, 1)])
    back = lax.all_to_all(back, "stream", 0, 0, tiled=True)
    dturn, vec, target, spread, uy = call(
        replay_kernel,
        [(SY, 5, SX, NN), (10, SX, NN), (128, 128), (128, 128), uy.shape],
        [cells, tile, tile, tile, cells, (SX * 5 * SY, NN), (SY, 5, 8, NN)],
        smem=1, vmem=5, hbm=5, sems=(8,), cost=4,
    )(node_count.reshape(1), back.reshape(XS * 8, NN), node_cell.reshape(1, -1), node_owner.reshape(1, -1),
      node_weight.reshape(1, -1), ly, in_hbm(driven), in_hbm(lx), in_hbm(ux), in_hbm(dy), in_hbm(uy))
    near = lax.ppermute(vec, "span", [(i, i ^ 1) for i in range(4)])
    (joint,) = call(join_kernel, [(5, SX, NN)], [], smem=1, vmem=4, cost=0.1)(z, vec, near, mats, other)
    beyond = lax.ppermute(joint, "span", [(i, 3 - i) for i in range(4)])
    new, part = call(
        finish_kernel,
        [list(cells), (128, NN)],
        [(5, SX, NN), (5, SX, NN), (SY, 5, SX, NN), (SY * 5 * SX, NN), (3, 128, NN), cells],
        sems=(1,), smem=1, vmem=13, cost=2,
    )(z, vec, near, beyond, mats, other, far, dturn, ly, uy, adjoint, metric, target, spread)
    parts = lax.all_to_all(part, ("stream", "span"), 0, 0, tiled=True)
    (control,) = call(sum_kernel, [(3, 16)], [], vmem=1)(parts)
    return new.transpose(0, 2, 1, 3), control


def solution(mesh):
    cells, mats = P("stream", "span", None, None), P("stream", "span", None, None, None)
    slots = P("stream", "span", None)
    return jax.shard_map(
        shards,
        mesh=mesh,
        in_specs=(cells,) * 2 + (mats,) * 7 + (slots,) * 3 + (P("stream", "span"),),
        out_specs=(cells, P(None, ("stream", "span"))),
        check_vma=False,
    )
```

```python
import jax
import jax.numpy as jnp
from jax import lax
from jax.experimental import pallas as pl
from jax.experimental.pallas import tpu as pltpu
from jax.sharding import PartitionSpec as P

SX, SY, NN = 16, 8, 128
XS = 32
ROWS = 24


def act(m, v):
    out = []
    for a in range(5):
        t = m[5 * a] * v[0]
        for b in range(1, 5):
            t = t + m[5 * a + b] * v[b]
        out.append(t)
    return out


def act_cols(m, f):
    cols = [act(m, [f[5 * b + c] for b in range(5)]) for c in range(5)]
    return [cols[c][a] for a in range(5) for c in range(5)]


def add(p, q):
    return [x + y for x, y in zip(p, q)]


def sub(p, q):
    return [x - y for x, y in zip(p, q)]


def lanes_quarter(shape):
    return lax.shift_right_logical(lax.broadcasted_iota(jnp.int32, shape, 1), 5)


def tiles(ref, i, n=25):
    return [ref[i, k] for k in range(n)]


def put(ref, i, vals):
    for k, v in enumerate(vals):
        ref[i, k] = v


def copies(pairs, sems):
    out = [pltpu.make_async_copy(src, dst, sems.at[k]) for k, (src, dst) in enumerate(pairs)]
    for c in out:
        c.start()
    return out


STEP = 4


def maps_kernel(rhs_h, dx_h, lx_h, ux_h, ly_h, uy_h, msg_h, driven_h, mats,
                lx, ux, rhs, dx, fs, gs, driven, msg, ly, uy, fy, sems):
    chunks = [pl.ds(k * STEP, STEP) for k in range(SX // STEP)]
    halves = [pl.ds(SX // 2, SX // 2), pl.ds(0, SX // 2)]
    pairs = [(ux_h.at[c], ux.at[c]) for c in halves]
    pairs += [(rhs_h, rhs)]
    for c in chunks:
        pairs += [(lx_h.at[c], lx.at[c]), (dx_h.at[c], dx.at[c])]
    late = len(pairs)
    pairs += [(ly_h, ly), (uy_h, uy)]
    flight = copies(pairs, sems)
    out_sem = len(pairs)

    def back_map(k, bm):
        return act_cols(tiles(ux, SX - 2 - k), bm)

    flight[0].wait()
    bm = lax.fori_loop(0, SX // 2 - 1, back_map, tiles(ux, SX - 1), unroll=True)
    flight[1].wait()
    bm = lax.fori_loop(SX // 2 - 1, SX - 1, back_map, bm, unroll=True)

    def fore(i, carry):
        g, f = carry
        l = tiles(lx, i)
        d = act(tiles(dx, i), tiles(rhs, i, 5))
        put(driven, i, d)
        g = sub(d, act(l, g))
        put(gs, i, g)
        f = act_cols(l, f)
        put(fs, i, f)
        return g, f

    for k in range(len(chunks)):
        for c in flight[3 + 2 * k : 5 + 2 * k]:
            c.wait()
        if k == 0:
            flight[2].wait()
            g = act(tiles(dx, 0), tiles(rhs, 0, 5))
            put(driven, 0, g)
            put(gs, 0, g)
            f = tiles(lx, 0)
            put(fs, 0, f)
        g, f = lax.fori_loop(max(1, STEP * k), STEP * k + STEP, fore, (g, f), unroll=True)
    kept = pltpu.make_async_copy(driven, driven_h, sems.at[out_sem])
    kept.start()

    def back(k, carry):
        i = SX - 2 - k
        b, c = carry
        u = tiles(ux, i)
        b = sub(tiles(gs, i, 5), act(u, b))
        c = add(tiles(fs, i), act_cols(u, c))
        return b, c

    b, c = lax.fori_loop(0, SX - 1, back, (g, f), unroll=3)
    zero = jnp.zeros((SY, NN), jnp.float32)
    values = f + g + bm + b + [-x for x in c] + [zero] * 3
    quarter = lanes_quarter((SY, NN))
    for r in range(22):
        four = values[4 * r : 4 * r + 4]
        for nq in range(4):
            out = None
            for kk in range(4):
                shift = (32 * (kk - nq)) % 128
                part = four[kk] if shift == 0 else pltpu.roll(four[kk], shift, 1)
                out = part if out is None else jnp.where(quarter == kk, part, out)
            msg[pl.ds(nq * 8 * ROWS + r, 8, ROWS), :] = out
    for r in range(22, ROWS):
        for nq in range(4):
            msg[pl.ds(nq * 8 * ROWS + r, 8, ROWS), :] = zero
    sent = pltpu.make_async_copy(msg, msg_h, sems.at[out_sem + 1])
    sent.start()

    def turned(ref, h, y):
        return [ref[pl.ds(h * 1600 + k * 8 + y, 8, 200), :] for k in range(25)]

    flight[late].wait()
    for h in range(2):
        f = turned(ly, h, 0)
        put(fy, 8 * h, f)

        def fore_y(y, f):
            f = act_cols(turned(ly, h, y), f)
            put(fy, 8 * h + y, f)
            return f

        f = lax.fori_loop(1, SY, fore_y, f, unroll=True)
        for k in range(25):
            mats[k, pl.ds(h * 8, 8), :] = f[k]
    flight[late + 1].wait()
    for h in range(2):
        def back_y(k, c):
            y = SY - 2 - k
            return add(tiles(fy, 8 * h + y), act_cols(turned(uy, h, y), c))

        c = lax.fori_loop(0, SY - 1, back_y, tiles(fy, 8 * h + SY - 1), unroll=True)
        for k in range(25):
            mats[50 + k, pl.ds(h * 8, 8), :] = -c[k]

        def back_map_y(k, bm):
            return act_cols(turned(uy, h, SY - 2 - k), bm)

        bm = lax.fori_loop(0, SY - 1, back_map_y, turned(uy, h, SY - 1), unroll=True)
        for k in range(25):
            mats[25 + k, pl.ds(h * 8, 8), :] = bm[k]
    sent.wait()
    kept.wait()


def solve_kernel(got, out, un, qs):
    un[0] = got[...]
    for q in range(1, 4):
        for p in range(XS):
            un[q, p] = pltpu.roll(got[p], 128 - 32 * q, 1)

    def val(p, k):
        return un[k % 4, p, (k // 4) : (k // 4) + 1, :]

    def keep(p, first, v):
        for j in range(5):
            k = first + j
            qs[k % 4, p, (k // 4) : (k // 4) + 1, :] = v[j]

    zero = [jnp.zeros((1, NN), jnp.float32)] * 5

    def fore(p, f):
        keep(p, 0, f)
        return add(act([val(p, k) for k in range(25)], f), [val(p, 25 + j) for j in range(5)])

    lax.fori_loop(0, XS, fore, zero, unroll=16)

    def back(k, s):
        p = XS - 1 - k
        keep(p, 5, s)
        f = [qs[j % 4, p, (j // 4) : (j // 4) + 1, :] for j in range(5)]
        known = add(act([val(p, 60 + k) for k in range(25)], f), [val(p, 55 + j) for j in range(5)])
        return add(known, act([val(p, 30 + k) for k in range(25)], s))

    lax.fori_loop(0, XS, back, zero, unroll=16)
    quarter = lanes_quarter((8, NN))
    for p in range(XS):
        t = qs[0, p]
        for q in range(1, 4):
            t = jnp.where(quarter == q, pltpu.roll(qs[q, p], 32 * q, 1), t)
        out[p] = t[:4]


def replay_kernel(count, got, cell, owner, weight, ly, driven_h, lx_h, ux_h, dy_h, uy_h, dturn, vec, target,
                  spread, uy, driven, lx, ux, dy, fs, sd, gt, sems):
    step = SX // 2
    halves = [pl.ds(0, step), pl.ds(step, step)]
    pairs = [(driven_h, driven)] + [(lx_h.at[c], lx.at[c]) for c in halves]
    for c in halves[::-1]:
        pairs += [(ux_h.at[c], ux.at[c]), (dy_h.at[c], dy.at[c])]
    flight = copies(pairs + [(uy_h, uy)], sems)

    row = lax.broadcasted_iota(jnp.int32, (128, 128), 0)
    lane = lax.broadcasted_iota(jnp.int32, (128, 128), 1)
    here = cell[...] == row
    used = jnp.logical_and(here, lane < count[0])
    w = jnp.sum(jnp.where(used, weight[...], 0.0), axis=1, keepdims=True)
    who = jnp.sum(jnp.where(here, owner[...].astype(jnp.float32), 0.0), axis=1, keepdims=True)
    who = who.astype(jnp.int32)
    target[...] = (lax.shift_right_logical(who, 4) == lane).astype(jnp.float32).T
    mine = jnp.logical_and(lane < 96, (lane & 15) == (who & 15))
    spread[...] = jnp.where(mine, w, 0.0)


    quarter = lanes_quarter((SY, NN))

    def entering(k):
        out = None
        for nq in range(4):
            part = got[pl.ds(nq * 32 + k // 4, 8, 4), :]
            shift = (32 * nq - 32 * (k % 4)) % 128
            part = part if shift == 0 else pltpu.roll(part, shift, 1)
            out = part if out is None else jnp.where(quarter == nq, part, out)
        return out

    def fore(i, f):
        f = sub(tiles(driven, i, 5), act(tiles(lx, i), f))
        for a in range(5):
            fs[i, a] = f[a]
        return f

    f = [entering(j) for j in range(5)]
    flight[0].wait()
    for k in range(2):
        flight[1 + k].wait()
        f = lax.fori_loop(step * k, step * k + step, fore, f, unroll=2)

    def back(k, s):
        i = SX - 1 - k
        s = sub(tiles(fs, i, 5), act(tiles(ux, i), s))
        d = act(tiles(dy, i), s)
        for a in range(5):
            sd[pl.ds(pl.multiple_of((i * 5 + a) * 8, 8), 8), :] = d[a]
        return s

    s = [entering(5 + j) for j in range(5)]
    for k in range(2):
        flight[3 + 2 * k].wait()
        flight[4 + 2 * k].wait()
        s = lax.fori_loop(step * k, step * k + step, back, s, unroll=2)
    flight[-1].wait()
    for h in range(2):
        def turned(ref, y):
            return [ref[pl.ds(h * 1600 + k * 8 + y, 8, 200), :] for k in range(25)]

        g = None
        for y in range(SY):
            d = [sd[pl.ds(h * 320 + a * 8 + y, 8, 40), :] for a in range(5)]
            for a in range(5):
                dturn[y, a, pl.ds(h * 8, 8), :] = d[a]
            g = d if g is None else sub(d, act(turned(ly, y), g))
            for a in range(5):
                gt[y, a] = g[a]
        for a in range(5):
            vec[a, pl.ds(h * 8, 8), :] = g[a]
        b = g
        for y in range(SY - 2, -1, -1):
            b = sub([gt[y, a] for a in range(5)], act(turned(uy, y), b))
        for a in range(5):
            vec[5 + a, pl.ds(h * 8, 8), :] = b[a]


HALVES = [pl.ds(0, 8), pl.ds(8, 8)]


def part_of(v, at, h, n=5):
    return [v[at + k, HALVES[h], :] for k in range(n)]


def by_side(z_ref, body):
    @pl.when((z_ref[0] & 1) == 0)
    def _():
        body(0, 1)

    @pl.when((z_ref[0] & 1) == 1)
    def _():
        body(1, 0)


def pair_kernel(z_ref, mats, other, out):
    m = [mats, other]

    def body(lo, up):
        for h in range(2):
            t = act_cols(part_of(m[up], 50, h, 25), part_of(m[lo], 0, h, 25))
            t = add(part_of(m[lo], 50, h, 25), act_cols(part_of(m[lo], 25, h, 25), t))
            for k in range(25):
                out[k, HALVES[h], :] = t[k]

    by_side(z_ref, body)


def join_kernel(z_ref, vec, near, mats, other, out):
    m, v = [mats, other], [vec, near]

    def body(lo, up):
        def put_out(h, t):
            for j in range(5):
                out[j, HALVES[h], :] = t[j]

        for h in range(2):
            @pl.when(z_ref[0] < 2)
            def _():
                put_out(h, add(part_of(v[up], 0, h), act(part_of(m[up], 0, h, 25), part_of(v[lo], 0, h))))

            @pl.when(z_ref[0] >= 2)
            def _():
                t = add(part_of(v[up], 5, h), act(part_of(m[up], 50, h, 25), part_of(v[lo], 0, h)))
                put_out(h, add(part_of(v[lo], 5, h), act(part_of(m[lo], 25, h, 25), t)))

    by_side(z_ref, body)


def finish_kernel(z_ref, vec, near, beyond, mats, other, far, dturn, ly, uy, adjoint, metric, target,
                  spread, new_h, part, fin, sin, ft, ut, pk, new, sems):
    z = z_ref[0]
    halves = HALVES
    zero = [jnp.zeros((8, NN), jnp.float32)] * 5

    def put_in(h, f):
        for j in range(5):
            fin[j, halves[h], :] = f[j]

    def put_back(h, s):
        for j in range(5):
            sin[j, halves[h], :] = s[j]

    for h in range(2):
        def lower(m1, a0, a1):
            f2 = add(a1, act(part_of(m1, 0, h, 25), a0))
            return add(part_of(beyond, 0, h), act(part_of(far, 0, h, 25), f2))

        @pl.when(z == 0)
        def _():
            put_in(h, zero)
            a0 = part_of(vec, 0, h)
            s2 = lower(other, a0, part_of(near, 0, h))
            s1 = add(part_of(near, 5, h), act(part_of(other, 50, h, 25), a0))
            put_back(h, add(s1, act(part_of(other, 25, h, 25), s2)))

        @pl.when(z == 1)
        def _():
            a0 = part_of(near, 0, h)
            put_in(h, a0)
            put_back(h, lower(mats, a0, part_of(vec, 0, h)))

        @pl.when(z == 2)
        def _():
            f2 = part_of(beyond, 0, h)
            put_in(h, f2)
            f3 = add(part_of(vec, 0, h), act(part_of(mats, 0, h, 25), f2))
            put_back(h, add(part_of(near, 5, h), act(part_of(other, 50, h, 25), f3)))

        @pl.when(z == 3)
        def _():
            put_in(h, add(part_of(near, 0, h), act(part_of(other, 0, h, 25), part_of(beyond, 0, h))))
            put_back(h, zero)

    def turned(ref, y, h):
        return [ref[pl.ds(h * 1600 + k * 8 + y, 8, 200), :] for k in range(25)]

    for h in range(2):
        f = [fin[j, halves[h], :] for j in range(5)]
        for y in range(SY):
            f = sub([dturn[y, a, halves[h], :] for a in range(5)], act(turned(ly, y, h), f))
            for a in range(5):
                ft[y, a, halves[h], :] = f[a]

    for h in range(2):
        s = [sin[j, halves[h], :] for j in range(5)]
        for y in range(SY - 1, -1, -1):
            s = sub([ft[y, a, halves[h], :] for a in range(5)], act(turned(uy, y, h), s))
            for a in range(5):
                ut[pl.ds((y * 5 + a) * 16 + h * 8, 8), :] = s[a]

    for x in range(SX):
        for a in range(5):
            new[x, a] = adjoint[x, a] + ut[pl.ds(a * 16 + x, 8, 80), :]
    sent = pltpu.make_async_copy(new, new_h, sems.at[0])
    sent.start()
    for x in range(SX):
        fresh = tiles(new, x, 5)
        for k in range(3):
            t = metric[x, 5 * k].astype(jnp.float32) * fresh[0]
            for a in range(1, 5):
                t = t + metric[x, 5 * k + a].astype(jnp.float32) * fresh[a]
            pk[k, pl.ds(x * 8, 8), :] = t

    group = lax.shift_right_logical(lax.broadcasted_iota(jnp.int32, (128, 128), 1), 4)
    value = jnp.zeros((128, 128), jnp.float32)
    for k in range(3):
        value = jnp.where(group % 3 == k, jnp.sum(pk[k], axis=1, keepdims=True), value)
    value = value * spread[...]
    high = value.astype(jnp.bfloat16).astype(jnp.float32)
    value = jnp.where(group < 3, high, value - high).astype(jnp.bfloat16)
    part[...] = jnp.dot(target[...].astype(jnp.bfloat16), value, preferred_element_type=jnp.float32)
    sent.wait()


def sum_kernel(parts, out):
    total = jnp.sum(parts[...], axis=0, keepdims=True)
    total = total + pltpu.roll(total, 80, 1)
    for k in range(3):
        part = total if k == 0 else pltpu.roll(total, 128 - 16 * k, 1)
        out[k : k + 1, :] = part[:, :16]


def call(kernel, outs, scratch, smem=0, vmem=0, hbm=0, sems=(), cost=0, limit=16):
    spec = pl.BlockSpec
    out_specs = [spec(memory_space=pltpu.HBM if isinstance(s, list) else pltpu.VMEM) for s in outs]
    return pl.pallas_call(
        kernel,
        out_shape=[pltpu.HBM(tuple(s), jnp.float32) if isinstance(s, list) else jax.ShapeDtypeStruct(s, jnp.float32)
                   for s in outs],
        in_specs=[spec(memory_space=pltpu.SMEM)] * smem + [spec(memory_space=pltpu.VMEM)] * vmem
        + [spec(memory_space=pltpu.HBM)] * hbm,
        out_specs=out_specs,
        scratch_shapes=[pltpu.VMEM(s, jnp.float32) for s in scratch]
        + [pltpu.SemaphoreType.DMA((n,)) for n in sems],
        compiler_params=pltpu.CompilerParams(vmem_limit_bytes=limit * 1024 * 1024),
        cost_estimate=pl.CostEstimate(flops=int(cost * 1e9), bytes_accessed=1000, transcendentals=0),
    )


def in_hbm(x):
    return pltpu.with_memory_space_constraint(x, pltpu.HBM)


def shards(rhs, adjoint, diag_x, lower_x, upper_x, diag_y, lower_y, upper_y, metric, node_cell,
           node_owner, node_weight, node_count):
    def blocks(m):
        return m.transpose(0, 2, 3, 1, 4).reshape(SX, -1, SY, NN)

    rhs = rhs.transpose(0, 2, 1, 3)
    adjoint = adjoint.transpose(0, 2, 1, 3)
    dx, lx, ux, dy = blocks(diag_x), blocks(lower_x), blocks(upper_x), blocks(diag_y)
    ly = blocks(lower_y).reshape(-1, NN)
    uy = blocks(upper_y).reshape(-1, NN)
    metric = blocks(metric)
    z = lax.axis_index("span").astype(jnp.int32).reshape(1)

    tile, cells, msg_shape = (SX, 25, SY, NN), (SX, 5, SY, NN), (XS * ROWS, NN)
    msg, driven, mats = call(
        maps_kernel,
        [list(msg_shape), list(cells), (75, SX, NN)],
        [tile, tile, cells, tile, tile, cells, cells, msg_shape, ly.shape, uy.shape, (2 * SY, 25, 8, NN)],
        hbm=6, sems=(15,), cost=7, limit=20,
    )(in_hbm(rhs), in_hbm(dx), in_hbm(lx), in_hbm(ux), in_hbm(ly), in_hbm(uy))
    got = lax.all_to_all(msg.reshape(XS, ROWS, NN), "stream", 0, 0, tiled=True)
    other = lax.ppermute(mats, "span", [(1, 0), (2, 3), (3, 2)])
    (back,) = call(
        solve_kernel, [(XS, 4, NN)],
        [(4, XS, ROWS, NN), (4, XS, 8, NN)], vmem=1, cost=12,
    )(got)
    (pair,) = call(pair_kernel, [(25, SX, NN)], [], smem=1, vmem=2, cost=0.2)(z, mats, other)
    far = lax.ppermute(pair, "span", [(3, 0), (2, 1)])
    back = lax.all_to_all(back, "stream", 0, 0, tiled=True)
    dturn, vec, target, spread, uy = call(
        replay_kernel,
        [(SY, 5, SX, NN), (10, SX, NN), (128, 128), (128, 128), uy.shape],
        [cells, tile, tile, tile, cells, (SX * 5 * SY, NN), (SY, 5, 8, NN)],
        smem=1, vmem=5, hbm=5, sems=(8,), cost=4,
    )(node_count.reshape(1), back.reshape(XS * 4, NN), node_cell.reshape(1, -1), node_owner.reshape(1, -1),
      node_weight.reshape(1, -1), ly, in_hbm(driven), in_hbm(lx), in_hbm(ux), in_hbm(dy), in_hbm(uy))
    near = lax.ppermute(vec, "span", [(i, i ^ 1) for i in range(4)])
    (joint,) = call(join_kernel, [(5, SX, NN)], [], smem=1, vmem=4, cost=0.1)(z, vec, near, mats, other)
    beyond = lax.ppermute(joint, "span", [(i, 3 - i) for i in range(4)])
    new, part = call(
        finish_kernel,
        [list(cells), (128, NN)],
        [(5, SX, NN), (5, SX, NN), (SY, 5, SX, NN), (SY * 5 * SX, NN), (3, 128, NN), cells],
        sems=(1,), smem=1, vmem=13, cost=2,
    )(z, vec, near, beyond, mats, other, far, dturn, ly, uy, adjoint, metric, target, spread)
    parts = lax.all_to_all(part, ("stream", "span"), 0, 0, tiled=True)
    (control,) = call(sum_kernel, [(3, 16)], [], vmem=1)(parts)
    return new.transpose(0, 2, 1, 3), control


def solution(mesh):
    cells, mats = P("stream", "span", None, None), P("stream", "span", None, None, None)
    slots = P("stream", "span", None)
    return jax.shard_map(
        shards,
        mesh=mesh,
        in_specs=(cells,) * 2 + (mats,) * 7 + (slots,) * 3 + (P("stream", "span"),),
        out_specs=(cells, P(None, ("stream", "span"))),
        check_vma=False,
    )
```

```python
import jax
import jax.numpy as jnp
from jax import lax
from jax.experimental import pallas as pl
from jax.experimental.pallas import tpu as pltpu
from jax.sharding import PartitionSpec as P

SX, SY, NN = 16, 8, 128
XS = 32
ROWS = 24


def act(m, v):
    out = []
    for a in range(5):
        t = m[5 * a] * v[0]
        for b in range(1, 5):
            t = t + m[5 * a + b] * v[b]
        out.append(t)
    return out


def act_cols(m, f):
    cols = [act(m, [f[5 * b + c] for b in range(5)]) for c in range(5)]
    return [cols[c][a] for a in range(5) for c in range(5)]


def add(p, q):
    return [x + y for x, y in zip(p, q)]


def sub(p, q):
    return [x - y for x, y in zip(p, q)]


def lanes_quarter(shape):
    return lax.shift_right_logical(lax.broadcasted_iota(jnp.int32, shape, 1), 5)


def tiles(ref, i, n=25):
    return [ref[i, k] for k in range(n)]


def put(ref, i, vals):
    for k, v in enumerate(vals):
        ref[i, k] = v


def copies(pairs, sems):
    out = [pltpu.make_async_copy(src, dst, sems.at[k]) for k, (src, dst) in enumerate(pairs)]
    for c in out:
        c.start()
    return out


STEP = 4


def maps_kernel(rhs_h, dx_h, lx_h, ux_h, ly_h, uy_h, msg_h, driven_h, mats,
                lx, ux, rhs, dx, fs, gs, driven, msg, ly, uy, fy, sems):
    chunks = [pl.ds(k * STEP, STEP) for k in range(SX // STEP)]
    halves = [pl.ds(SX // 2, SX // 2), pl.ds(0, SX // 2)]
    pairs = [(ux_h.at[c], ux.at[c]) for c in halves]
    pairs += [(rhs_h, rhs)]
    for c in chunks:
        pairs += [(lx_h.at[c], lx.at[c]), (dx_h.at[c], dx.at[c])]
    late = len(pairs)
    pairs += [(ly_h, ly), (uy_h, uy)]
    flight = copies(pairs, sems)
    out_sem = len(pairs)

    def back_map(k, bm):
        return act_cols(tiles(ux, SX - 2 - k), bm)

    flight[0].wait()
    bm = lax.fori_loop(0, SX // 2 - 1, back_map, tiles(ux, SX - 1), unroll=True)
    flight[1].wait()
    bm = lax.fori_loop(SX // 2 - 1, SX - 1, back_map, bm, unroll=True)

    def fore(i, carry):
        g, f = carry
        l = tiles(lx, i)
        d = act(tiles(dx, i), tiles(rhs, i, 5))
        put(driven, i, d)
        g = sub(d, act(l, g))
        put(gs, i, g)
        f = act_cols(l, f)
        put(fs, i, f)
        return g, f

    for k in range(len(chunks)):
        for c in flight[3 + 2 * k : 5 + 2 * k]:
            c.wait()
        if k == 0:
            flight[2].wait()
            g = act(tiles(dx, 0), tiles(rhs, 0, 5))
            put(driven, 0, g)
            put(gs, 0, g)
            f = tiles(lx, 0)
            put(fs, 0, f)
        g, f = lax.fori_loop(max(1, STEP * k), STEP * k + STEP, fore, (g, f), unroll=True)
    kept = pltpu.make_async_copy(driven, driven_h, sems.at[out_sem])
    kept.start()

    def back(k, carry):
        i = SX - 2 - k
        b, c = carry
        u = tiles(ux, i)
        b = sub(tiles(gs, i, 5), act(u, b))
        c = add(tiles(fs, i), act_cols(u, c))
        return b, c

    b, c = lax.fori_loop(0, SX - 1, back, (g, f), unroll=3)
    zero = jnp.zeros((SY, NN), jnp.float32)
    values = f + g + bm + b + [-x for x in c] + [zero] * 3
    quarter = lanes_quarter((SY, NN))
    for r in range(22):
        four = values[4 * r : 4 * r + 4]
        for nq in range(4):
            out = None
            for kk in range(4):
                shift = (32 * (kk - nq)) % 128
                part = four[kk] if shift == 0 else pltpu.roll(four[kk], shift, 1)
                out = part if out is None else jnp.where(quarter == kk, part, out)
            msg[pl.ds(nq * 8 * ROWS + r, 8, ROWS), :] = out
    for r in range(22, ROWS):
        for nq in range(4):
            msg[pl.ds(nq * 8 * ROWS + r, 8, ROWS), :] = zero
    sent = pltpu.make_async_copy(msg, msg_h, sems.at[out_sem + 1])
    sent.start()

    def turned(ref, h, y):
        return [ref[pl.ds(h * 1600 + k * 8 + y, 8, 200), :] for k in range(25)]

    flight[late].wait()
    for h in range(2):
        f = turned(ly, h, 0)
        put(fy, 8 * h, f)

        def fore_y(y, f):
            f = act_cols(turned(ly, h, y), f)
            put(fy, 8 * h + y, f)
            return f

        f = lax.fori_loop(1, SY, fore_y, f, unroll=True)
        for k in range(25):
            mats[k, pl.ds(h * 8, 8), :] = f[k]
    flight[late + 1].wait()
    for h in range(2):
        def back_y(k, c):
            y = SY - 2 - k
            return add(tiles(fy, 8 * h + y), act_cols(turned(uy, h, y), c))

        c = lax.fori_loop(0, SY - 1, back_y, tiles(fy, 8 * h + SY - 1), unroll=True)
        for k in range(25):
            mats[50 + k, pl.ds(h * 8, 8), :] = -c[k]

        def back_map_y(k, bm):
            return act_cols(turned(uy, h, SY - 2 - k), bm)

        bm = lax.fori_loop(0, SY - 1, back_map_y, turned(uy, h, SY - 1), unroll=True)
        for k in range(25):
            mats[25 + k, pl.ds(h * 8, 8), :] = bm[k]
    sent.wait()
    kept.wait()


def solve_kernel(got, out, un, qs):
    un[0] = got[...]
    for q in range(1, 4):
        for p in range(XS):
            un[q, p] = pltpu.roll(got[p], 128 - 32 * q, 1)

    def val(p, k):
        return un[k % 4, p, (k // 4) : (k // 4) + 1, :]

    def keep(p, first, v):
        for j in range(5):
            k = first + j
            qs[k % 4, p, (k // 4) : (k // 4) + 1, :] = v[j]

    zero = [jnp.zeros((1, NN), jnp.float32)] * 5

    def fore(p, f):
        keep(p, 0, f)
        return add(act([val(p, k) for k in range(25)], f), [val(p, 25 + j) for j in range(5)])

    lax.fori_loop(0, XS, fore, zero, unroll=True)

    def back(k, s):
        p = XS - 1 - k
        keep(p, 5, s)
        f = [qs[j % 4, p, (j // 4) : (j // 4) + 1, :] for j in range(5)]
        known = add(act([val(p, 60 + k) for k in range(25)], f), [val(p, 55 + j) for j in range(5)])
        return add(known, act([val(p, 30 + k) for k in range(25)], s))

    lax.fori_loop(0, XS, back, zero, unroll=True)
    quarter = lanes_quarter((8, NN))
    for p in range(XS):
        t = qs[0, p]
        for q in range(1, 4):
            t = jnp.where(quarter == q, pltpu.roll(qs[q, p], 32 * q, 1), t)
        out[p] = t[:4]


def replay_kernel(count, got, cell, owner, weight, ly, driven_h, lx_h, ux_h, dy_h, uy_h, dturn, vec, target,
                  spread, uy, driven, lx, ux, dy, fs, sd, gt, sems):
    step = SX // 2
    halves = [pl.ds(0, step), pl.ds(step, step)]
    pairs = [(driven_h, driven)] + [(lx_h.at[c], lx.at[c]) for c in halves]
    for c in halves[::-1]:
        pairs += [(ux_h.at[c], ux.at[c]), (dy_h.at[c], dy.at[c])]
    flight = copies(pairs + [(uy_h, uy)], sems)

    row = lax.broadcasted_iota(jnp.int32, (128, 128), 0)
    lane = lax.broadcasted_iota(jnp.int32, (128, 128), 1)
    here = cell[...] == row
    used = jnp.logical_and(here, lane < count[0])
    w = jnp.sum(jnp.where(used, weight[...], 0.0), axis=1, keepdims=True)
    who = jnp.sum(jnp.where(here, owner[...].astype(jnp.float32), 0.0), axis=1, keepdims=True)
    who = who.astype(jnp.int32)
    target[...] = (lax.shift_right_logical(who, 4) == lane).astype(jnp.float32).T
    mine = jnp.logical_and(lane < 96, (lane & 15) == (who & 15))
    spread[...] = jnp.where(mine, w, 0.0)


    quarter = lanes_quarter((SY, NN))

    def entering(k):
        out = None
        for nq in range(4):
            part = got[pl.ds(nq * 32 + k // 4, 8, 4), :]
            shift = (32 * nq - 32 * (k % 4)) % 128
            part = part if shift == 0 else pltpu.roll(part, shift, 1)
            out = part if out is None else jnp.where(quarter == nq, part, out)
        return out

    def fore(i, f):
        f = sub(tiles(driven, i, 5), act(tiles(lx, i), f))
        for a in range(5):
            fs[i, a] = f[a]
        return f

    f = [entering(j) for j in range(5)]
    flight[0].wait()
    for k in range(2):
        flight[1 + k].wait()
        f = lax.fori_loop(step * k, step * k + step, fore, f, unroll=2)

    def back(k, s):
        i = SX - 1 - k
        s = sub(tiles(fs, i, 5), act(tiles(ux, i), s))
        d = act(tiles(dy, i), s)
        for a in range(5):
            sd[pl.ds(pl.multiple_of((i * 5 + a) * 8, 8), 8), :] = d[a]
        return s

    s = [entering(5 + j) for j in range(5)]
    for k in range(2):
        flight[3 + 2 * k].wait()
        flight[4 + 2 * k].wait()
        s = lax.fori_loop(step * k, step * k + step, back, s, unroll=2)
    flight[-1].wait()
    for h in range(2):
        def turned(ref, y):
            return [ref[pl.ds(h * 1600 + k * 8 + y, 8, 200), :] for k in range(25)]

        g = None
        for y in range(SY):
            d = [sd[pl.ds(h * 320 + a * 8 + y, 8, 40), :] for a in range(5)]
            for a in range(5):
                dturn[y, a, pl.ds(h * 8, 8), :] = d[a]
            g = d if g is None else sub(d, act(turned(ly, y), g))
            for a in range(5):
                gt[y, a] = g[a]
        for a in range(5):
            vec[a, pl.ds(h * 8, 8), :] = g[a]
        b = g
        for y in range(SY - 2, -1, -1):
            b = sub([gt[y, a] for a in range(5)], act(turned(uy, y), b))
        for a in range(5):
            vec[5 + a, pl.ds(h * 8, 8), :] = b[a]


HALVES = [pl.ds(0, 8), pl.ds(8, 8)]


def part_of(v, at, h, n=5):
    return [v[at + k, HALVES[h], :] for k in range(n)]


def by_side(z_ref, body):
    @pl.when((z_ref[0] & 1) == 0)
    def _():
        body(0, 1)

    @pl.when((z_ref[0] & 1) == 1)
    def _():
        body(1, 0)


def pair_kernel(z_ref, mats, other, out):
    m = [mats, other]

    def body(lo, up):
        for h in range(2):
            t = act_cols(part_of(m[up], 50, h, 25), part_of(m[lo], 0, h, 25))
            t = add(part_of(m[lo], 50, h, 25), act_cols(part_of(m[lo], 25, h, 25), t))
            for k in range(25):
                out[k, HALVES[h], :] = t[k]

    by_side(z_ref, body)


def join_kernel(z_ref, vec, near, mats, other, out):
    m, v = [mats, other], [vec, near]

    def body(lo, up):
        def put_out(h, t):
            for j in range(5):
                out[j, HALVES[h], :] = t[j]

        for h in range(2):
            @pl.when(z_ref[0] < 2)
            def _():
                put_out(h, add(part_of(v[up], 0, h), act(part_of(m[up], 0, h, 25), part_of(v[lo], 0, h))))

            @pl.when(z_ref[0] >= 2)
            def _():
                t = add(part_of(v[up], 5, h), act(part_of(m[up], 50, h, 25), part_of(v[lo], 0, h)))
                put_out(h, add(part_of(v[lo], 5, h), act(part_of(m[lo], 25, h, 25), t)))

    by_side(z_ref, body)


def finish_kernel(z_ref, vec, near, beyond, mats, other, far, dturn, ly, uy, adjoint, metric, target,
                  spread, new_h, part, fin, sin, ft, ut, pk, new, sems):
    z = z_ref[0]
    halves = HALVES
    zero = [jnp.zeros((8, NN), jnp.float32)] * 5

    def put_in(h, f):
        for j in range(5):
            fin[j, halves[h], :] = f[j]

    def put_back(h, s):
        for j in range(5):
            sin[j, halves[h], :] = s[j]

    for h in range(2):
        def lower(m1, a0, a1):
            f2 = add(a1, act(part_of(m1, 0, h, 25), a0))
            return add(part_of(beyond, 0, h), act(part_of(far, 0, h, 25), f2))

        @pl.when(z == 0)
        def _():
            put_in(h, zero)
            a0 = part_of(vec, 0, h)
            s2 = lower(other, a0, part_of(near, 0, h))
            s1 = add(part_of(near, 5, h), act(part_of(other, 50, h, 25), a0))
            put_back(h, add(s1, act(part_of(other, 25, h, 25), s2)))

        @pl.when(z == 1)
        def _():
            a0 = part_of(near, 0, h)
            put_in(h, a0)
            put_back(h, lower(mats, a0, part_of(vec, 0, h)))

        @pl.when(z == 2)
        def _():
            f2 = part_of(beyond, 0, h)
            put_in(h, f2)
            f3 = add(part_of(vec, 0, h), act(part_of(mats, 0, h, 25), f2))
            put_back(h, add(part_of(near, 5, h), act(part_of(other, 50, h, 25), f3)))

        @pl.when(z == 3)
        def _():
            put_in(h, add(part_of(near, 0, h), act(part_of(other, 0, h, 25), part_of(beyond, 0, h))))
            put_back(h, zero)

    def turned(ref, y, h):
        return [ref[pl.ds(h * 1600 + k * 8 + y, 8, 200), :] for k in range(25)]

    for h in range(2):
        f = [fin[j, halves[h], :] for j in range(5)]
        for y in range(SY):
            f = sub([dturn[y, a, halves[h], :] for a in range(5)], act(turned(ly, y, h), f))
            for a in range(5):
                ft[y, a, halves[h], :] = f[a]

    for h in range(2):
        s = [sin[j, halves[h], :] for j in range(5)]
        for y in range(SY - 1, -1, -1):
            s = sub([ft[y, a, halves[h], :] for a in range(5)], act(turned(uy, y, h), s))
            for a in range(5):
                ut[pl.ds((y * 5 + a) * 16 + h * 8, 8), :] = s[a]

    for x in range(SX):
        for a in range(5):
            new[x, a] = adjoint[x, a] + ut[pl.ds(a * 16 + x, 8, 80), :]
    sent = pltpu.make_async_copy(new, new_h, sems.at[0])
    sent.start()
    for x in range(SX):
        fresh = tiles(new, x, 5)
        for k in range(3):
            t = metric[x, 5 * k].astype(jnp.float32) * fresh[0]
            for a in range(1, 5):
                t = t + metric[x, 5 * k + a].astype(jnp.float32) * fresh[a]
            pk[k, pl.ds(x * 8, 8), :] = t

    group = lax.shift_right_logical(lax.broadcasted_iota(jnp.int32, (128, 128), 1), 4)
    value = jnp.zeros((128, 128), jnp.float32)
    for k in range(3):
        value = jnp.where(group % 3 == k, jnp.sum(pk[k], axis=1, keepdims=True), value)
    value = value * spread[...]
    high = value.astype(jnp.bfloat16).astype(jnp.float32)
    value = jnp.where(group < 3, high, value - high).astype(jnp.bfloat16)
    part[...] = jnp.dot(target[...].astype(jnp.bfloat16), value, preferred_element_type=jnp.float32)
    sent.wait()


def sum_kernel(parts, out):
    total = jnp.sum(parts[...], axis=0, keepdims=True)
    total = total + pltpu.roll(total, 80, 1)
    for k in range(3):
        part = total if k == 0 else pltpu.roll(total, 128 - 16 * k, 1)
        out[k : k + 1, :] = part[:, :16]


def call(kernel, outs, scratch, smem=0, vmem=0, hbm=0, sems=(), cost=0, limit=16):
    spec = pl.BlockSpec
    out_specs = [spec(memory_space=pltpu.HBM if isinstance(s, list) else pltpu.VMEM) for s in outs]
    return pl.pallas_call(
        kernel,
        out_shape=[pltpu.HBM(tuple(s), jnp.float32) if isinstance(s, list) else jax.ShapeDtypeStruct(s, jnp.float32)
                   for s in outs],
        in_specs=[spec(memory_space=pltpu.SMEM)] * smem + [spec(memory_space=pltpu.VMEM)] * vmem
        + [spec(memory_space=pltpu.HBM)] * hbm,
        out_specs=out_specs,
        scratch_shapes=[pltpu.VMEM(s, jnp.float32) for s in scratch]
        + [pltpu.SemaphoreType.DMA((n,)) for n in sems],
        compiler_params=pltpu.CompilerParams(vmem_limit_bytes=limit * 1024 * 1024),
        cost_estimate=pl.CostEstimate(flops=int(cost * 1e9), bytes_accessed=1000, transcendentals=0),
    )


def in_hbm(x):
    return pltpu.with_memory_space_constraint(x, pltpu.HBM)


def shards(rhs, adjoint, diag_x, lower_x, upper_x, diag_y, lower_y, upper_y, metric, node_cell,
           node_owner, node_weight, node_count):
    def blocks(m):
        return m.transpose(0, 2, 3, 1, 4).reshape(SX, -1, SY, NN)

    rhs = rhs.transpose(0, 2, 1, 3)
    adjoint = adjoint.transpose(0, 2, 1, 3)
    dx, lx, ux, dy = blocks(diag_x), blocks(lower_x), blocks(upper_x), blocks(diag_y)
    ly = blocks(lower_y).reshape(-1, NN)
    uy = blocks(upper_y).reshape(-1, NN)
    metric = blocks(metric)
    z = lax.axis_index("span").astype(jnp.int32).reshape(1)

    tile, cells, msg_shape = (SX, 25, SY, NN), (SX, 5, SY, NN), (XS * ROWS, NN)
    msg, driven, mats = call(
        maps_kernel,
        [list(msg_shape), list(cells), (75, SX, NN)],
        [tile, tile, cells, tile, tile, cells, cells, msg_shape, ly.shape, uy.shape, (2 * SY, 25, 8, NN)],
        hbm=6, sems=(15,), cost=7, limit=20,
    )(in_hbm(rhs), in_hbm(dx), in_hbm(lx), in_hbm(ux), in_hbm(ly), in_hbm(uy))
    got = lax.all_to_all(msg.reshape(XS, ROWS, NN), "stream", 0, 0, tiled=True)
    other = lax.ppermute(mats, "span", [(1, 0), (2, 3), (3, 2)])
    (back,) = call(
        solve_kernel, [(XS, 4, NN)],
        [(4, XS, ROWS, NN), (4, XS, 8, NN)], vmem=1, cost=12,
    )(got)
    (pair,) = call(pair_kernel, [(25, SX, NN)], [], smem=1, vmem=2, cost=0.2)(z, mats, other)
    far = lax.ppermute(pair, "span", [(3, 0), (2, 1)])
    back = lax.all_to_all(back, "stream", 0, 0, tiled=True)
    dturn, vec, target, spread, uy = call(
        replay_kernel,
        [(SY, 5, SX, NN), (10, SX, NN), (128, 128), (128, 128), uy.shape],
        [cells, tile, tile, tile, cells, (SX * 5 * SY, NN), (SY, 5, 8, NN)],
        smem=1, vmem=5, hbm=5, sems=(8,), cost=4,
    )(node_count.reshape(1), back.reshape(XS * 4, NN), node_cell.reshape(1, -1), node_owner.reshape(1, -1),
      node_weight.reshape(1, -1), ly, in_hbm(driven), in_hbm(lx), in_hbm(ux), in_hbm(dy), in_hbm(uy))
    near = lax.ppermute(vec, "span", [(i, i ^ 1) for i in range(4)])
    (joint,) = call(join_kernel, [(5, SX, NN)], [], smem=1, vmem=4, cost=0.1)(z, vec, near, mats, other)
    beyond = lax.ppermute(joint, "span", [(i, 3 - i) for i in range(4)])
    new, part = call(
        finish_kernel,
        [list(cells), (128, NN)],
        [(5, SX, NN), (5, SX, NN), (SY, 5, SX, NN), (SY * 5 * SX, NN), (3, 128, NN), cells],
        sems=(1,), smem=1, vmem=13, cost=2,
    )(z, vec, near, beyond, mats, other, far, dturn, ly, uy, adjoint, metric, target, spread)
    parts = lax.all_to_all(part, ("stream", "span"), 0, 0, tiled=True)
    (control,) = call(sum_kernel, [(3, 16)], [], vmem=1)(parts)
    return new.transpose(0, 2, 1, 3), control


def solution(mesh):
    cells, mats = P("stream", "span", None, None), P("stream", "span", None, None, None)
    slots = P("stream", "span", None)
    return jax.shard_map(
        shards,
        mesh=mesh,
        in_specs=(cells,) * 2 + (mats,) * 7 + (slots,) * 3 + (P("stream", "span"),),
        out_specs=(cells, P(None, ("stream", "span"))),
        check_vma=False,
    )
```
